128 devices in a mesh: space: 16 (over z_hi, x, core), cuts: 8 (over z_lo, y).
Axes of the slice: x: 4, y: 4, z: 4 (z_hi: 2, z_lo: 2; z = z_hi * 2 + z_lo), core: 2. Of those that a mesh axis runs over, the one named last changes fastest.
Arguments:
- velocity: float32 [8, 3, 256, 128, 256], P('cuts', None, 'space'), may hold values from -2.5 to 2.5
- atlas_image: float32 [256, 128, 256], P('space', 'cuts'), may hold values from -6 to 6
- target: float32 [256, 128, 256], P('space', 'cuts'), may hold values from -6 to 6
- labels: int32 [256, 128, 256], P('space', 'cuts'), may hold values from 0 to 63
- label_table: float32 [64], replicated, may hold values from -1 to 1
- counts: int32 [128], P(('space', 'cuts')), may hold values from 16384 to 65536, as said below
Outputs:
- gradient: float32 [8, 3, 256, 128, 256], P('cuts', None, 'space')
The draws below stay inside these ranges and needn't reach their ends.
Inputs may be any that keep to these rules, and one draw needn't show every extreme that they name: counts[k] belongs to the tile of mesh position k, space-major; the masked voxels of a tile are its first counts[k] voxels in first, second, third dimension order.
All inputs are finite; a program needn't handle non-finite values.
Results may differ from the reference program's by a relative error of at most 0.0003.
Values sent between devices are 32-bit elements; how exact they have to be, the bound alone decides.
No kernel may reach another device: no remote copies, remote signals or barrier semaphores. Data moves between devices by JAX's collectives and lax.ppermute only.
A program may use at most 128 MiB of HBM per device.

```python
import jax
import jax.numpy as jnp
from jax import lax

CX = 16
CY = 16
NZ = 256
NT = 8
SMOOTH = 2
LABELS = 64
NX = 256
NY = 128
CELLS = 65536
TILES = 128
N_SPACE = 16
N_CUTS = 8


def draw_counts(key, part):
    key = jax.random.fold_in(key, 11)
    order = jnp.arange(TILES, dtype=jnp.int32)
    base = CELLS // 4 + 3 * CELLS // 4 * order // max(TILES - 1, 1)
    jitter = jax.random.randint(key, (TILES,), 0, CELLS // 8 + 1, dtype=jnp.int32)
    return jnp.minimum(base + jitter, CELLS).astype(jnp.int32)


def with_ends(values, rng, smallest, high):
    longest = values.shape.index(max(values.shape))
    spots = []
    for shift in (0, 1):
        where = [jax.random.randint(jax.random.fold_in(rng, axis), (), 0, length) for axis, length in enumerate(values.shape)]
        where[longest] = (where[longest] + shift) % values.shape[longest]
        spots.append(tuple(where))
    return values.at[spots[0]].set(smallest).at[spots[1]].set(high)


def block_scale(rng, extent, cuts, low, top_value):
    level, own = 1.0, jax.random.fold_in(rng, 6)
    for axis_at, parts in cuts:
        draws = jnp.exp(jax.random.uniform(jax.random.fold_in(own, axis_at), (parts,), jnp.float32, low / len(cuts), top_value / len(cuts)))
        level = level * jnp.repeat(draws, extent[axis_at] // parts).reshape([-1 if axis == axis_at else 1 for axis in range(len(extent))])
    return level


def centred(rng, shape, width, most, split=(), held_as=jnp.bfloat16):
    drawn = width * jax.random.normal(rng, shape, jnp.float32)
    if split:
        drawn = drawn * block_scale(rng, shape, split, -0.22, 0.18)
    return jnp.clip(drawn, -most, most).astype(held_as)


def setup_inputs(seed: int = 0) -> dict:
    keys = jax.random.split(jax.random.key(seed), 7)
    return {
        "velocity": centred(keys[0], (NT, 3, NX, NY, NZ), 0.8, 2.5, ((0, 8), (2, 16)), jnp.float32),
        "atlas_image": centred(keys[1], (NX, NY, NZ), 1.0, 6.0, ((0, 16), (1, 8)), jnp.float32),
        "target": centred(keys[2], (NX, NY, NZ), 1.0, 6.0, ((0, 16), (1, 8)), jnp.float32),
        "labels": with_ends(jax.random.randint(keys[3], (NX, NY, NZ), 0, LABELS), jax.random.fold_in(keys[3], 1), 0, LABELS - 1).astype(jnp.int32),
        "label_table": jnp.clip(jax.random.uniform(keys[4], (LABELS,), jnp.float32, -1.0, 1.0), -1.0, 1.0),
        "counts": draw_counts(jax.random.fold_in(keys[6], 71), 0),
    }


DATA_WEIGHT = 4.0
KAPPA = 0.125


def zero_border(volume):
    return jnp.pad(volume, [(0, 0)] * (volume.ndim - 3) + [(1, 1)] * 3)


def differences(padded):
    middle = padded[..., 1:-1, 1:-1, 1:-1]
    behind = [padded[..., :-2, 1:-1, 1:-1], padded[..., 1:-1, :-2, 1:-1], padded[..., 1:-1, 1:-1, :-2]]
    beyond = [padded[..., 2:, 1:-1, 1:-1], padded[..., 1:-1, 2:, 1:-1], padded[..., 1:-1, 1:-1, 2:]]
    return middle, behind, beyond


def advance(intensity_pad, velocity_now, time_step):
    middle, behind, beyond = differences(intensity_pad)
    outflow = jnp.zeros_like(middle)
    for direction in range(3):
        outflow = outflow + jnp.maximum(velocity_now[direction], 0.0) * (middle - behind[direction]) + jnp.minimum(velocity_now[direction], 0.0) * (beyond[direction] - middle)
    return middle - time_step * outflow


def sensitivity(intensity_pad, velocity_now, costate, time_step):
    middle, behind, beyond = differences(intensity_pad)
    pieces = []
    for direction in range(3):
        slope = jnp.where(velocity_now[direction] > 0.0, middle - behind[direction], beyond[direction] - middle)
        pieces.append(-time_step * costate * slope)
    return jnp.stack(pieces)


def transposed(costate_pad, velocity_pad, time_step):
    forward_part = jnp.maximum(velocity_pad, 0.0) * costate_pad[None]
    backward_part = jnp.minimum(velocity_pad, 0.0) * costate_pad[None]
    middle_now = costate_pad[1:-1, 1:-1, 1:-1]
    change = jnp.zeros_like(middle_now)
    for direction in range(3):
        f_middle, f_behind, f_beyond = differences(forward_part[direction])
        b_middle, b_behind, b_beyond = differences(backward_part[direction])
        change = change + (f_middle - f_beyond[direction]) + (b_behind[direction] - b_middle)
    return middle_now - time_step * change


def diffuse(padded):
    middle, behind, beyond = differences(padded)
    neighbours = behind[0] + beyond[0] + behind[1] + beyond[1] + behind[2] + beyond[2]
    return middle + KAPPA * (neighbours - 6.0 * middle)


def lookup_labels(labels, label_table):
    template = jnp.zeros(labels.shape, label_table.dtype)
    for label_value in range(label_table.shape[0]):
        template = template + jnp.where(labels == label_value, label_table[label_value], 0.0)
    return template


def tile_positions(rows, cols, depth):
    first = lax.broadcasted_iota(jnp.int32, (rows, cols, depth), 0) * (cols * depth)
    second = lax.broadcasted_iota(jnp.int32, (rows, cols, depth), 1) * depth
    return first + second + lax.broadcasted_iota(jnp.int32, (rows, cols, depth), 2)


def reference(velocity, atlas_image, target, labels, label_table, counts):
    time_step = 1.0 / NT
    intensity = atlas_image + lookup_labels(labels, label_table)
    positions = tile_positions(CX, CY, NZ)
    tile_counts = counts.reshape(N_SPACE, N_CUTS)
    inside = positions[None, None] < tile_counts[:, :, None, None, None]
    masked = jnp.transpose(inside, (0, 2, 1, 3, 4)).reshape(NX, NY, NZ).astype(jnp.float32)
    weighting = (NX * NY * NZ) / jnp.sum(counts.astype(jnp.float32))
    states = []
    for moment in range(NT):
        padded = zero_border(intensity)
        states.append(padded)
        intensity = advance(padded, velocity[moment], time_step)
    costate = DATA_WEIGHT * weighting * masked * (intensity - target)
    gradients = [None] * NT
    for moment in range(NT - 1, -1, -1):
        gradients[moment] = sensitivity(states[moment], velocity[moment], costate, time_step)
        if moment > 0:
            costate = transposed(zero_border(costate), zero_border(velocity[moment]), time_step)
    smoothed = jnp.stack(gradients)
    for sweep in range(SMOOTH):
        smoothed = diffuse(zero_border(smoothed))
    return velocity + smoothed
```

```python
import functools

import jax
import jax.numpy as jnp
from jax import lax
from jax.experimental import pallas as pl
from jax.experimental.pallas import tpu as pltpu
from jax.sharding import PartitionSpec as P

F32 = jnp.float32
NT = 8
STEP = 1.0 / NT
DATA_WEIGHT = 4.0
KAPPA = 0.125
CX, CY, NZ = 16, 16, 256
NY = 128
DEPTH = 4
WX, WY = CX + 2 * DEPTH, CY + 2 * DEPTH
V_SLOTS = ((0, 3, 0), (1, 2, 3), (2, 1, 5))
V_ROWS = 6
VX = CX + 6
VMEM = pltpu.VMEM
ANY = pl.ANY


def whole():
    return pl.BlockSpec(memory_space=VMEM)


def anywhere():
    return pl.BlockSpec(memory_space=ANY)


def scalars():
    return pl.BlockSpec(memory_space=pltpu.SMEM)


def params():
    return pltpu.CompilerParams(vmem_limit_bytes=56 * 1024 * 1024)


def sds(*shape):
    return jax.ShapeDtypeStruct(shape, F32)


def swaps(size, first):
    pairs = []
    for i in range(first, size - 1, 2):
        pairs += [(i, i + 1), (i + 1, i)]
    return pairs


def swap(even, odd, axis):
    size = lax.axis_size(axis)
    return lax.ppermute(even, axis, swaps(size, 0)), lax.ppermute(odd, axis, swaps(size, 1))


def total_of(value):
    for axis in ("cuts", "space"):
        size = lax.axis_size(axis)
        reach = 1
        while reach < size:
            value = value + lax.ppermute(value, axis, [(i, i ^ reach) for i in range(size)])
            reach *= 2
    return value


def rows8():
    return lax.broadcasted_iota(jnp.int32, (8, NZ), 0)


def turn(block, shift):
    shift = shift % 8
    return pltpu.roll(block, shift, 0) if shift else block


def put(total, block, shift, low, high, sub):
    return jnp.where((sub >= low) & (sub < high), turn(block, shift), total)


def pack_edges(slots, tile, sub):
    top = jnp.zeros((8, NZ), F32)
    bottom = top
    for key, k, off in slots:
        low8, high8 = tile(key)
        top = put(top, high8, off + k, off, off + k, sub)
        bottom = put(bottom, low8, off, off, off + k, sub)
    return top, bottom


def halo_block(above, below, k, off, sub):
    block = put(jnp.zeros((8, NZ), F32), above, -off, 0, k, sub)
    return put(block, below, 8 - k - off, 8 - k, 8, sub)


def lane_masks(shape):
    z = lax.broadcasted_iota(jnp.int32, shape, 1)
    return z == 0, z == NZ - 1


def copies(pairs, sem):
    started = [pltpu.make_async_copy(a, b, sem.at[i]) for i, (a, b) in enumerate(pairs)]
    for copy in started:
        copy.start()
    return started


def wait_all(started):
    for copy in started:
        copy.wait()


def fill_velocity(group, info, vt, ra, rb, yc, yd, vw, sem):
    px, py = info[2], info[3]
    pairs = []
    for j in range(4):
        pairs.append((vt.at[4 * group + j], vw.at[j, :, 0:CX, 0:CY]))
    for j, k, off in V_SLOTS:
        to_a = jnp.where(px == 0, CX, WX - k)
        to_b = jnp.where(px == 0, WX - k, CX)
        pairs.append((ra.at[group, :, off : off + k], vw.at[j, :, pl.ds(to_a, k), 0:CY]))
        pairs.append((rb.at[group, :, off : off + k], vw.at[j, :, pl.ds(to_b, k), 0:CY]))
    started = copies(pairs, sem)
    sub = rows8()
    zero_row = jnp.zeros((WY, NZ), F32)
    zero_tile = jnp.zeros((8, NZ), F32)
    for j in range(4):
        k = 3 - j
        for d in range(3):
            for x in range(CX + k, WX - k):
                vw[j, d, x] = zero_row

    def one(i, carry):
        x = jnp.where(i < CX + 3, i, i + 2)
        for d in range(3):
            c, e = yc[d, i], yd[d, i]
            above = jnp.where(py == 0, c, e)
            below = jnp.where(py == 0, e, c)
            for j, k, off in V_SLOTS:
                vw[j, d, x, CY:WY] = halo_block(above, below, k, off, sub)
            vw[3, d, x, CY:WY] = zero_tile
        return carry

    lax.fori_loop(0, CX, one, 0)
    for i in range(CX, VX):
        x = i if i < CX + 3 else i + 2
        for d in range(3):
            c, e = yc[d, i], yd[d, i]
            above = jnp.where(py == 0, c, e)
            below = jnp.where(py == 0, e, c)
            for j, k, off in V_SLOTS:
                if x < CX + k or x >= WX - k:
                    vw[j, d, x, CY:WY] = halo_block(above, below, k, off, sub)
    return started


def fill_image(info, win, yc, yd, image):
    py = info[3]
    sub = rows8()

    def one(i, carry):
        c, e = yc[i], yd[i]
        above = jnp.where(py == 0, c, e)
        below = jnp.where(py == 0, e, c)
        image[i, 0:CY] = win[i]
        image[i + 12, 0:CY] = win[i + 12]
        image[i, CY:WY] = halo_block(above, below, 4, 0, sub)
        image[i + 12, CY:WY] = halo_block(above, below, 4, 4, sub)
        return carry

    lax.fori_loop(0, 12, one, 0)


def advance(src, dst, vw, j, reach):
    first, last = lane_masks((WY, NZ))

    def one(i, carry):
        x = lax.rem(i - reach + WX, WX)
        xm = lax.rem(x + WX - 1, WX)
        xp = lax.rem(x + 1, WX)
        c = src[x]
        v0, v1, v2 = vw[j, 0, x], vw[j, 1, x], vw[j, 2, x]
        flow = v0 * jnp.where(v0 > 0.0, c - src[xm], src[xp] - c)
        flow += v1 * jnp.where(v1 > 0.0, c - pltpu.roll(c, 1, 0), pltpu.roll(c, WY - 1, 0) - c)
        behind = jnp.where(first, 0.0, pltpu.roll(c, 1, 1))
        beyond = jnp.where(last, 0.0, pltpu.roll(c, NZ - 1, 1))
        flow += v2 * jnp.where(v2 > 0.0, c - behind, beyond - c)
        dst[x] = c - STEP * flow
        return carry

    lax.fori_loop(0, CX + 2 * reach, one, 0)


def scatter(src, dst, vw, j, reach):
    first, last = lane_masks((WY, NZ))

    def one(i, carry):
        x = lax.rem(i - reach + WX, WX)
        xm = lax.rem(x + WX - 1, WX)
        xp = lax.rem(x + 1, WX)
        c = src[x]
        v0, v1, v2 = vw[j, 0, x], vw[j, 1, x], vw[j, 2, x]
        change = (jnp.abs(v0) + jnp.abs(v1) + jnp.abs(v2)) * c
        change -= jnp.maximum(vw[j, 0, xp], 0.0) * src[xp]
        change += jnp.minimum(vw[j, 0, xm], 0.0) * src[xm]
        change -= pltpu.roll(jnp.maximum(v1, 0.0) * c, WY - 1, 0)
        change += pltpu.roll(jnp.minimum(v1, 0.0) * c, 1, 0)
        change -= jnp.where(last, 0.0, pltpu.roll(jnp.maximum(v2, 0.0) * c, NZ - 1, 1))
        change += jnp.where(first, 0.0, pltpu.roll(jnp.minimum(v2, 0.0) * c, 1, 1))
        dst[x] = c - STEP * change
        return carry

    lax.fori_loop(0, CX + 2 * reach, one, 0)


def clear_halo(ref, x_rows=True):
    zero_row = jnp.zeros((WY, NZ), F32)
    for x in range(CX, WX):
        ref[x] = zero_row


def repack(velocity):
    def kernel(src, dst, sem):
        pairs = []
        for c in range(NY // CY):
            for d in range(3):
                pairs.append((src.at[0, d, :, c * CY : (c + 1) * CY], dst.at[c, d]))
        wait_all(copies(pairs, sem))

    return pl.pallas_call(
        kernel,
        out_shape=sds(NY // CY, 3, CX, CY, NZ),
        in_specs=[anywhere()],
        out_specs=anywhere(),
        scratch_shapes=[pltpu.SemaphoreType.DMA((24,))],
        compiler_params=params(),
    )(velocity)


def template(info, table, atlas, labels):
    def kernel(info, table, atlas, labels, tmpl, ea, eb):
        def one(x, carry):
            lab = labels[x]
            value = jnp.zeros((CY, NZ), F32)
            for l in range(64):
                value = jnp.where(lab == l, table[l], value)
            tmpl[x] = atlas[x] + value
            return carry

        lax.fori_loop(0, CX, one, 0)
        px = info[2]
        ea[...] = tmpl[pl.ds(jnp.where(px == 0, CX - DEPTH, 0), DEPTH)]
        eb[...] = tmpl[pl.ds(jnp.where(px == 0, 0, CX - DEPTH), DEPTH)]

    return pl.pallas_call(
        kernel,
        out_shape=[sds(CX, CY, NZ), sds(DEPTH, CY, NZ), sds(DEPTH, CY, NZ)],
        in_specs=[scalars(), scalars(), whole(), whole()],
        out_specs=[whole()] * 3,
        compiler_params=params(),
    )(info, table, atlas, labels)


def image_edges(info, tile, ra, rb):
    def kernel(info, tile, ra, rb, win, ec, ed):
        px, py = info[2], info[3]
        win[0:CX] = tile[...]
        win[pl.ds(jnp.where(px == 0, CX, WX - DEPTH), DEPTH)] = ra[...]
        win[pl.ds(jnp.where(px == 0, WX - DEPTH, CX), DEPTH)] = rb[...]
        sub = rows8()

        def one(i, carry):
            def tile_of(key):
                return win[i + key, 0:8], win[i + key, 8:16]

            top, bottom = pack_edges(((0, 4, 0), (12, 4, 4)), tile_of, sub)
            ec[i] = jnp.where(py == 0, top, bottom)
            ed[i] = jnp.where(py == 0, bottom, top)
            return carry

        lax.fori_loop(0, 12, one, 0)

    return pl.pallas_call(
        kernel,
        out_shape=[sds(WX, CY, NZ), sds(12, 8, NZ), sds(12, 8, NZ)],
        in_specs=[scalars()] + [whole()] * 3,
        out_specs=[whole()] * 3,
        compiler_params=params(),
    )(info, tile, ra, rb)


def velocity_faces(info, vt):
    def kernel(info, vt, ea, eb, sem):
        px = info[2]
        pairs = []
        for g in range(2):
            for j, k, off in V_SLOTS:
                top = jnp.where(px == 0, CX - k, 0)
                bottom = jnp.where(px == 0, 0, CX - k)
                pairs.append((vt.at[4 * g + j, :, pl.ds(top, k)], ea.at[g, :, off : off + k]))
                pairs.append((vt.at[4 * g + j, :, pl.ds(bottom, k)], eb.at[g, :, off : off + k]))
        wait_all(copies(pairs, sem))

    return pl.pallas_call(
        kernel,
        out_shape=[sds(2, 3, V_ROWS, CY, NZ)] * 2,
        in_specs=[scalars(), anywhere()],
        out_specs=[anywhere()] * 2,
        scratch_shapes=[pltpu.SemaphoreType.DMA((12,))],
        compiler_params=params(),
    )(info, vt)


def velocity_edges(info, vt, ra, rb, group):
    def kernel(info, vt, ra, rb, ec, ed):
        px, py = info[2], info[3]
        sub = rows8()

        def emit(i, slots, tile_of):
            top, bottom = pack_edges(slots, tile_of, sub)
            ec[0, i] = jnp.where(py == 0, top, bottom)
            ed[0, i] = jnp.where(py == 0, bottom, top)

        def one(x, carry):
            emit(x, V_SLOTS, lambda j: (vt[j, 0, x, 0:8], vt[j, 0, x, 8:16]))
            return carry

        lax.fori_loop(0, CX, one, 0)
        for i in range(3):
            up, down = [], []
            for j, k, off in V_SLOTS:
                if i < k:
                    up.append((j, k, off))
                if i >= 3 - k:
                    down.append((j, k, off))

            def tile_up(j):
                row = V_SLOTS[j][2] + i
                a, b = ra[0, 0, row], rb[0, 0, row]
                value = jnp.where(px == 0, a, b)
                return value[0:8], value[8:16]

            def tile_down(j):
                row = V_SLOTS[j][2] + i - (3 - V_SLOTS[j][1])
                a, b = ra[0, 0, row], rb[0, 0, row]
                value = jnp.where(px == 0, b, a)
                return value[0:8], value[8:16]

            emit(CX + i, up, tile_up)
            emit(CX + 3 + i, down, tile_down)

    return pl.pallas_call(
        kernel,
        grid=(3,),
        out_shape=[sds(3, VX, 8, NZ)] * 2,
        in_specs=[
            scalars(),
            pl.BlockSpec((4, 1, CX, CY, NZ), lambda d: (group, d, 0, 0, 0)),
            pl.BlockSpec((1, 1, V_ROWS, CY, NZ), lambda d: (group, d, 0, 0, 0)),
            pl.BlockSpec((1, 1, V_ROWS, CY, NZ), lambda d: (group, d, 0, 0, 0)),
        ],
        out_specs=[pl.BlockSpec((1, VX, 8, NZ), lambda d: (d, 0, 0, 0))] * 2,
        compiler_params=params(),
    )(info, vt, ra, rb)


def forward_first(info, win, ic, idd, vt, ra, rb, yc, yd):
    def kernel(info, win, ic, idd, vt, ra, rb, yc, yd, states, ea, eb, i4, vw, image, sem, osem):
        started = fill_velocity(0, info, vt, ra, rb, yc, yd, vw, sem)
        fill_image(info, win, ic, idd, image.at[0])
        wait_all(started)
        out = []
        for j in range(4):
            advance(image.at[j], image.at[j + 1], vw, j, 3 - j)
            out.append(pltpu.make_async_copy(image.at[j, 0:CX, 0:CY], states.at[j], osem.at[j]))
            out[-1].start()
        px = info[2]
        last = image.at[4]
        i4[...] = last[0:CX, 0:CY]
        ea[...] = last[pl.ds(jnp.where(px == 0, CX - DEPTH, 0), DEPTH), 0:CY]
        eb[...] = last[pl.ds(jnp.where(px == 0, 0, CX - DEPTH), DEPTH), 0:CY]
        wait_all(out)

    return pl.pallas_call(
        kernel,
        out_shape=[sds(NT, CX, CY, NZ), sds(DEPTH, CY, NZ), sds(DEPTH, CY, NZ), sds(CX, CY, NZ)],
        in_specs=[scalars()] + [whole()] * 3 + [anywhere()] * 3 + [whole()] * 2,
        out_specs=[anywhere()] + [whole()] * 3,
        scratch_shapes=[
            VMEM((4, 3, WX, WY, NZ), F32),
            VMEM((5, WX, WY, NZ), F32),
            pltpu.SemaphoreType.DMA((10,)),
            pltpu.SemaphoreType.DMA((4,)),
        ],
        compiler_params=params(),
    )(info, win, ic, idd, vt, ra, rb, yc, yd)


def send_rows(info, widths, source, ea, eb):
    px = info[2]
    off = 0
    for n, k in enumerate(widths):
        top = jnp.where(px == 0, CX, WX - k)
        bottom = jnp.where(px == 0, WX - k, CX)
        ea[off : off + k] = source(n)[pl.ds(top, k)]
        eb[off : off + k] = source(n)[pl.ds(bottom, k)]
        off += k


MID_WIDTHS = (4, 3, 2, 1)
MID_SLOTS = ((0, 4, 0), (1, 3, 4), (3, 1, 7))
END_WIDTHS = (3, 2, 1)
END_SLOTS = ((0, 3, 0), (1, 2, 3), (2, 1, 5), (3, 2, 6))


def forward_second(info, win, ic, idd, target, vt, ra, rb, yc, yd, states):
    def kernel(info, win, ic, idd, target, vt, ra, rb, yc, yd, states_in, states, costates, lw, ea, eb, vw, image, lam, sem, osem):
        started = fill_velocity(1, info, vt, ra, rb, yc, yd, vw, sem)
        fill_image(info, win, ic, idd, image.at[0])
        for n in range(4):
            clear_halo(lam.at[n])
        wait_all(started)
        out = []
        for j in range(4):
            advance(image.at[j], image.at[j + 1], vw, j, 3 - j)
            out.append(pltpu.make_async_copy(image.at[j, 0:CX, 0:CY], states.at[4 + j], osem.at[j]))
            out[-1].start()
        count = info[4]
        inside = lax.broadcasted_iota(jnp.int32, (CY, NZ), 0) * NZ + lax.broadcasted_iota(jnp.int32, (CY, NZ), 1)
        zero = jnp.zeros((8, NZ), F32)

        def one(x, carry):
            value = image[4, x, 0:CY] - target[x]
            lam[0, x, 0:CY] = jnp.where(inside + x * (CY * NZ) < count, value, 0.0)
            lam[0, x, CY:WY] = zero
            return carry

        lax.fori_loop(0, CX, one, 0)
        out.append(pltpu.make_async_copy(lam.at[0, 0:CX, 0:CY], costates.at[7], osem.at[4]))
        out[-1].start()
        for n in range(4):
            scatter(lam.at[n], lam.at[n + 1], vw, 3 - n, n + 1)
        for n in range(4):
            lw[n] = lam[4 - n, 0:CX]
        send_rows(info, MID_WIDTHS, lambda n: lam.at[4 - n], ea, eb)
        wait_all(out)

    return pl.pallas_call(
        kernel,
        out_shape=[
            sds(NT, CX, CY, NZ),
            sds(NT, CX, CY, NZ),
            sds(4, CX, WY, NZ),
            sds(10, WY, NZ),
            sds(10, WY, NZ),
        ],
        in_specs=[scalars()] + [whole()] * 4 + [anywhere()] * 3 + [whole()] * 2 + [anywhere()],
        out_specs=[anywhere()] * 2 + [whole()] * 3,
        scratch_shapes=[
            VMEM((4, 3, WX, WY, NZ), F32),
            VMEM((5, WX, WY, NZ), F32),
            VMEM((5, WX, WY, NZ), F32),
            pltpu.SemaphoreType.DMA((10,)),
            pltpu.SemaphoreType.DMA((5,)),
        ],
        input_output_aliases={10: 0},
        compiler_params=params(),
    )(info, win, ic, idd, target, vt, ra, rb, yc, yd, states)


def costate_edges(info, lw, ra, rb, widths, slots):
    def kernel(info, lw_in, ra, rb, lw, ec, ed):
        px, py = info[2], info[3]
        lw[...] = lw_in[...]
        off = 0
        for n, k in enumerate(widths):
            for i in range(k):
                to_a = jnp.where(px == 0, CX - k, 0) + i
                to_b = jnp.where(px == 0, 0, CX - k) + i
                lw[n, to_a] = lw[n, to_a] + ra[off + i]
                lw[n, to_b] = lw[n, to_b] + rb[off + i]
            off += k
        sub = rows8()

        def one(x, carry):
            top = jnp.zeros((8, NZ), F32)
            bottom = top
            for n, k, off in slots:
                block = lw[n, x, CY:WY]
                top = put(top, block, off, off, off + k, sub)
                bottom = put(bottom, block, off + k, off, off + k, sub)
            ec[x] = jnp.where(py == 0, top, bottom)
            ed[x] = jnp.where(py == 0, bottom, top)
            return carry

        lax.fori_loop(0, CX, one, 0)

    return pl.pallas_call(
        kernel,
        out_shape=[sds(4, CX, WY, NZ), sds(CX, 8, NZ), sds(CX, 8, NZ)],
        in_specs=[scalars()] + [whole()] * 3,
        out_specs=[whole()] * 3,
        compiler_params=params(),
    )(info, lw, ra, rb)


def take(c, e, py, k, off, sub):
    below = jnp.where(py == 0, e, c)
    above = jnp.where(py == 0, c, e)
    zero = jnp.zeros((8, NZ), F32)
    return put(zero, below, -off, 0, k, sub), put(zero, above, 8 - k - off, 8 - k, 8, sub)


def backward_second(info, lw, lc, ld, vt, ra, rb, yc, yd, costates):
    def kernel(info, lw, lc, ld, vt, ra, rb, yc, yd, costates_in, costates, lw2, ea, eb, vw, lam, done, sem, osem):
        started = fill_velocity(0, info, vt, ra, rb, yc, yd, vw, sem)
        for n in range(3):
            clear_halo(lam.at[n])
        py = info[3]
        sub = rows8()
        zero = jnp.zeros((8, NZ), F32)

        def one(x, carry):
            c, e = lc[x], ld[x]
            for n, k, off in MID_SLOTS:
                low, high = take(c, e, py, k, off, sub)
                low, high = lw[n, x, 0:8] + low, lw[n, x, 8:16] + high
                if n == 0:
                    lam[0, x, 0:8] = low
                    lam[0, x, 8:16] = high
                    lam[0, x, CY:WY] = zero
                else:
                    done[(n - 1) // 2, x, 0:8] = low
                    done[(n - 1) // 2, x, 8:16] = high
            return carry

        lax.fori_loop(0, CX, one, 0)
        out = [
            pltpu.make_async_copy(lam.at[0, 0:CX, 0:CY], costates.at[3], osem.at[0]),
            pltpu.make_async_copy(done.at[0], costates.at[4], osem.at[1]),
            pltpu.make_async_copy(done.at[1], costates.at[6], osem.at[2]),
        ]
        for copy in out:
            copy.start()
        wait_all(started)
        for n in range(3):
            scatter(lam.at[n], lam.at[n + 1], vw, 3 - n, n + 1)
        for n in range(3):
            lw2[n] = lam[3 - n, 0:CX]
        lw2[3] = lw[2]
        send_rows(info, END_WIDTHS, lambda n: lam.at[3 - n], ea, eb)
        wait_all(out)

    return pl.pallas_call(
        kernel,
        out_shape=[sds(NT, CX, CY, NZ), sds(4, CX, WY, NZ), sds(6, WY, NZ), sds(6, WY, NZ)],
        in_specs=[scalars()] + [whole()] * 3 + [anywhere()] * 3 + [whole()] * 2 + [anywhere()],
        out_specs=[anywhere()] + [whole()] * 3,
        scratch_shapes=[
            VMEM((4, 3, WX, WY, NZ), F32),
            VMEM((4, WX, WY, NZ), F32),
            VMEM((2, CX, CY, NZ), F32),
            pltpu.SemaphoreType.DMA((10,)),
            pltpu.SemaphoreType.DMA((3,)),
        ],
        input_output_aliases={9: 0},
        compiler_params=params(),
    )(info, lw, lc, ld, vt, ra, rb, yc, yd, costates)


def costate_finish(info, lw, lc, ld, costates):
    def kernel(info, lw, lc, ld, costates_in, costates, done, sem):
        py = info[3]
        sub = rows8()

        def one(x, carry):
            c, e = lc[x], ld[x]
            for n, k, off in END_SLOTS:
                low, high = take(c, e, py, k, off, sub)
                done[n, x, 0:8] = lw[n, x, 0:8] + low
                done[n, x, 8:16] = lw[n, x, 8:16] + high
            return carry

        lax.fori_loop(0, CX, one, 0)
        wait_all(copies([(done.at[n], costates.at[m]) for n, m in enumerate((0, 1, 2, 5))], sem))

    return pl.pallas_call(
        kernel,
        out_shape=sds(NT, CX, CY, NZ),
        in_specs=[scalars()] + [whole()] * 3 + [anywhere()],
        out_specs=anywhere(),
        scratch_shapes=[VMEM((4, CX, CY, NZ), F32), pltpu.SemaphoreType.DMA((4,))],
        input_output_aliases={4: 0},
        compiler_params=params(),
    )(info, lw, lc, ld, costates)


def finish(info, weight, velocity, va, vb, image, ia, ib, costate, la, lb):
    def kernel(info, weight, vel, va, vb, image, ia, ib, costate, la, lb, out, islab, lslab, grad, soft, sem):
        d = pl.program_id(0)
        px = info[2]
        coef = weight[0]

        @pl.when(d == 0)
        def _():
            pairs = []
            i_a, i_b = jnp.where(px == 0, CX + 3, 0), jnp.where(px == 0, 0, CX + 3)
            l_a, l_b = jnp.where(px == 0, CX + 2, 0), jnp.where(px == 0, 0, CX + 2)
            for c in range(NY // CY):
                y = slice(c * CY, (c + 1) * CY)
                pairs += [
                    (image.at[c], islab.at[3 : CX + 3, y]),
                    (ia.at[c], islab.at[pl.ds(i_a, 3), y]),
                    (ib.at[c], islab.at[pl.ds(i_b, 3), y]),
                    (costate.at[c], lslab.at[2 : CX + 2, y]),
                    (la.at[c], lslab.at[pl.ds(l_a, 2), y]),
                    (lb.at[c], lslab.at[pl.ds(l_b, 2), y]),
                ]
            wait_all(copies(pairs, sem))

        first, last = lane_masks((NY, NZ))
        y = lax.broadcasted_iota(jnp.int32, (NY, NZ), 0)
        bottom, top = y == 0, y == NY - 1

        def row(r, v, direction):
            c = islab[r + 1]
            if direction == 0:
                behind, beyond = islab[r], islab[r + 2]
            elif direction == 1:
                behind = jnp.where(bottom, 0.0, pltpu.roll(c, 1, 0))
                beyond = jnp.where(top, 0.0, pltpu.roll(c, NY - 1, 0))
            else:
                behind = jnp.where(first, 0.0, pltpu.roll(c, 1, 1))
                beyond = jnp.where(last, 0.0, pltpu.roll(c, NZ - 1, 1))
            slope = jnp.where(v > 0.0, c - behind, beyond - c)
            grad[r] = (coef * lslab[r]) * slope

        for direction in range(3):

            @pl.when(d == direction)
            def _(direction=direction):
                for i in range(2):
                    row(i, jnp.where(px == 0, vb[0, i], va[0, i]), direction)
                    row(CX + 2 + i, jnp.where(px == 0, va[0, i], vb[0, i]), direction)

                def one(x, carry):
                    row(x + 2, vel[0, 0, x], direction)
                    return carry

                lax.fori_loop(0, CX, one, 0)

        def sweep(ref, r):
            c = ref[r]
            near = ref[r - 1] + ref[r + 1]
            near += jnp.where(bottom, 0.0, pltpu.roll(c, 1, 0)) + jnp.where(top, 0.0, pltpu.roll(c, NY - 1, 0))
            near += jnp.where(first, 0.0, pltpu.roll(c, 1, 1)) + jnp.where(last, 0.0, pltpu.roll(c, NZ - 1, 1))
            return c + KAPPA * (near - 6.0 * c)

        def once(r, carry):
            soft[r] = sweep(grad, r + 1)
            return carry

        lax.fori_loop(0, CX + 2, once, 0)
        zero = jnp.zeros((NY, NZ), F32)

        @pl.when(info[0] == 0)
        def _():
            soft[0] = zero

        @pl.when(info[0] == info[5] - 1)
        def _():
            soft[CX + 1] = zero

        def twice(x, carry):
            out[0, 0, x] = vel[0, 0, x] + sweep(soft, x + 1)
            return carry

        lax.fori_loop(0, CX, twice, 0)

    face = pl.BlockSpec((1, 2, NY, NZ), lambda d: (d, 0, 0, 0))
    slab = pl.BlockSpec((1, 1, CX, NY, NZ), lambda d: (0, d, 0, 0, 0))
    return pl.pallas_call(
        kernel,
        grid=(3,),
        out_shape=sds(1, 3, CX, NY, NZ),
        in_specs=[scalars(), scalars(), slab, face, face] + [anywhere()] * 6,
        out_specs=slab,
        scratch_shapes=[
            VMEM((CX + 6, NY, NZ), F32),
            VMEM((CX + 4, NY, NZ), F32),
            VMEM((CX + 4, NY, NZ), F32),
            VMEM((CX + 2, NY, NZ), F32),
            pltpu.SemaphoreType.DMA((48,)),
        ],
        compiler_params=params(),
    )(info, weight, velocity, va, vb, image, ia, ib, costate, la, lb)


def edge_rows(value, dim, k, px):
    length = value.shape[dim]
    high = lax.slice_in_dim(value, length - k, length, axis=dim)
    low = lax.slice_in_dim(value, 0, k, axis=dim)
    return jnp.where(px == 0, high, low), jnp.where(px == 0, low, high)


def shards(velocity, atlas_image, target, labels, label_table, counts):
    s, c = lax.axis_index("space"), lax.axis_index("cuts")
    px, py = s % 2, c % 2
    info = jnp.stack([s, c, px, py, counts[0], jnp.int32(lax.axis_size("space")), s, s]).astype(jnp.int32)
    tiled = lax.all_to_all(repack(velocity), "cuts", split_axis=0, concat_axis=0, tiled=True)

    total = total_of(jnp.broadcast_to(counts.astype(F32)[:, None], (1, 128)))[0, 0]
    cells = CX * CY * NZ * lax.axis_size("space") * lax.axis_size("cuts")
    weight = jnp.reshape(-STEP * DATA_WEIGHT * (cells / total), (1,)).astype(F32)
    tile, ea, eb = template(info, label_table, atlas_image, labels)
    win, ec, ed = image_edges(info, tile, *swap(ea, eb, "space"))
    ic, idd = swap(ec, ed, "cuts")
    ova, ovb = edge_rows(velocity[0], 1, 2, px)
    ova, ovb = swap(ova, ovb, "space")

    fa, fb = velocity_faces(info, tiled)
    fa, fb = swap(fa, fb, "space")
    y0 = swap(*velocity_edges(info, tiled, fa, fb, 0), "cuts")
    y1 = swap(*velocity_edges(info, tiled, fa, fb, 1), "cuts")

    states, ea, eb, i4 = forward_first(info, win, ic, idd, tiled, fa, fb, *y0)
    win, ec, ed = image_edges(info, i4, *swap(ea, eb, "space"))
    ic, idd = swap(ec, ed, "cuts")
    states, costates, lw, ea, eb = forward_second(info, win, ic, idd, target, tiled, fa, fb, *y1, states)
    image = lax.all_to_all(states, "cuts", split_axis=0, concat_axis=0, tiled=True)
    lw, ec, ed = costate_edges(info, lw, *swap(ea, eb, "space"), MID_WIDTHS, MID_SLOTS)
    ec, ed = swap(ec, ed, "cuts")
    costates, lw, ea, eb = backward_second(info, lw, ec, ed, tiled, fa, fb, *y0, costates)
    lw, ec, ed = costate_edges(info, lw, *swap(ea, eb, "space"), END_WIDTHS, END_SLOTS)
    ec, ed = swap(ec, ed, "cuts")
    costates = costate_finish(info, lw, ec, ed, costates)
    costate = lax.all_to_all(costates, "cuts", split_axis=0, concat_axis=0, tiled=True)

    ia, ib = swap(*edge_rows(image, 1, 3, px), "space")
    la, lb = swap(*edge_rows(costate, 1, 2, px), "space")
    return finish(info, weight, velocity, ova, ovb, image, ia, ib, costate, la, lb)


def solution(mesh):
    in_specs = (
        P("cuts", None, "space", None, None),
        P("space", "cuts", None),
        P("space", "cuts", None),
        P("space", "cuts", None),
        P(),
        P(("space", "cuts")),
    )
    out_specs = P("cuts", None, "space", None, None)
    return jax.shard_map(shards, mesh=mesh, in_specs=in_specs, out_specs=out_specs, check_vma=False)
```

```python
import functools

import jax
import jax.numpy as jnp
from jax import lax
from jax.experimental import pallas as pl
from jax.experimental.pallas import tpu as pltpu
from jax.sharding import PartitionSpec as P

F32 = jnp.float32
NT = 8
STEP = 1.0 / NT
DATA_WEIGHT = 4.0
KAPPA = 0.125
CX, CY, NZ = 16, 16, 256
NY = 128
DEPTH = 4
WX, WY = CX + 2 * DEPTH, CY + 2 * DEPTH
V_SLOTS = ((0, 3, 0), (1, 2, 3), (2, 1, 5))
V_ROWS = 6
VX = CX + 6
VBLOCKS = 3 * CX + 1
FACE = 2 * 3 * V_ROWS
VMEM = pltpu.VMEM
ANY = pl.ANY


def whole():
    return pl.BlockSpec(memory_space=VMEM)


def anywhere():
    return pl.BlockSpec(memory_space=ANY)


def scalars():
    return pl.BlockSpec(memory_space=pltpu.SMEM)


def params(mib=28):
    return pltpu.CompilerParams(vmem_limit_bytes=mib * 1024 * 1024)


def sds(*shape):
    return jax.ShapeDtypeStruct(shape, F32)


def swaps(size, first):
    pairs = []
    for i in range(first, size - 1, 2):
        pairs += [(i, i + 1), (i + 1, i)]
    return pairs


def swap(even, odd, axis):
    size = lax.axis_size(axis)
    return lax.ppermute(even, axis, swaps(size, 0)), lax.ppermute(odd, axis, swaps(size, 1))


def xor_swap(value, reach):
    size = lax.axis_size("space")
    return value + lax.ppermute(value, "space", [(i, i ^ reach) for i in range(size)])


def rows8():
    return lax.broadcasted_iota(jnp.int32, (8, NZ), 0)


def turn(block, shift):
    shift = shift % 8
    return pltpu.roll(block, shift, 0) if shift else block


def put(total, block, shift, low, high, sub):
    return jnp.where((sub >= low) & (sub < high), turn(block, shift), total)


def pack_edges(slots, tile, sub):
    top = jnp.zeros((8, NZ), F32)
    bottom = top
    for key, k, off in slots:
        low8, high8 = tile(key)
        top = put(top, high8, off + k, off, off + k, sub)
        bottom = put(bottom, low8, off, off, off + k, sub)
    return top, bottom


def halo_block(above, below, k, off, sub):
    block = put(jnp.zeros((8, NZ), F32), above, -off, 0, k, sub)
    return put(block, below, 8 - k - off, 8 - k, 8, sub)


def lane_masks(shape):
    z = lax.broadcasted_iota(jnp.int32, shape, 1)
    return z == 0, z == NZ - 1


def copies(pairs, sem):
    started = [pltpu.make_async_copy(a, b, sem.at[i]) for i, (a, b) in enumerate(pairs)]
    for copy in started:
        copy.start()
    return started


def wait_all(started):
    for copy in started:
        copy.wait()


def fill_velocity(group, info, vt, ra, rb, yc, yd, vw, sem):
    px, py = info[2], info[3]
    pairs = []
    for d in range(3):
        for j in range(4):
            pairs.append((vt.at[4 * group + j, d * CX : (d + 1) * CX], vw.at[j, d, 0:CX, 0:CY]))
        for j, k, off in V_SLOTS:
            to_a = jnp.where(px == 0, CX, WX - k)
            to_b = jnp.where(px == 0, WX - k, CX)
            row = (group * 3 + d) * V_ROWS + off
            pairs.append((ra.at[row : row + k], vw.at[j, d, pl.ds(to_a, k), 0:CY]))
            pairs.append((rb.at[row : row + k], vw.at[j, d, pl.ds(to_b, k), 0:CY]))
    started = copies(pairs, sem)
    sub = rows8()
    zero_row = jnp.zeros((WY, NZ), F32)
    zero_tile = jnp.zeros((8, NZ), F32)
    for j in range(4):
        k = 3 - j
        for d in range(3):
            for x in range(CX + k, WX - k):
                vw[j, d, x] = zero_row

    def blocks(d, i, x, keep):
        c, e = yc[d, i], yd[d, i]
        above = jnp.where(py == 0, c, e)
        below = jnp.where(py == 0, e, c)
        for j, k, off in V_SLOTS:
            if keep(k):
                vw[j, d, x, CY:WY] = halo_block(above, below, k, off, sub)

    def one(i, carry):
        for d in range(3):
            for r in range(2):
                blocks(d, 2 * i + r, 2 * i + r, lambda k: True)
                vw[3, d, 2 * i + r, CY:WY] = zero_tile
        return carry

    lax.fori_loop(0, CX // 2, one, 0)
    for i in range(CX, VX):
        x = i if i < CX + 3 else i + 2
        for d in range(3):
            blocks(d, i, x, lambda k: x < CX + k or x >= WX - k)
    return started


FILL_COPIES = 30


def fill_image(info, win, yc, yd, image):
    py = info[3]
    sub = rows8()

    def one(i, carry):
        c, e = yc[i], yd[i]
        above = jnp.where(py == 0, c, e)
        below = jnp.where(py == 0, e, c)
        image[i, 0:CY] = win[i]
        image[i + 12, 0:CY] = win[i + 12]
        image[i, CY:WY] = halo_block(above, below, 4, 0, sub)
        image[i + 12, CY:WY] = halo_block(above, below, 4, 4, sub)
        return carry

    lax.fori_loop(0, 12, one, 0)


ROWS = 2


def sweep_rows(reach, row, dst):
    turns = -(-(CX + 2 * reach) // ROWS)

    def one(i, carry):
        xs = [lax.rem(i * ROWS + r - reach + WX, WX) for r in range(ROWS)]
        values = [row(x, lax.rem(x + WX - 1, WX), lax.rem(x + 1, WX)) for x in xs]
        for x, value in zip(xs, values):
            dst[x] = value
        return carry

    lax.fori_loop(0, turns, one, 0)


def advance(src, dst, vw, j, reach):
    first, last = lane_masks((WY, NZ))

    def row(x, xm, xp):
        c = src[x]
        v0, v1, v2 = vw[j, 0, x], vw[j, 1, x], vw[j, 2, x]
        flow = v0 * jnp.where(v0 > 0.0, c - src[xm], src[xp] - c)
        flow += v1 * jnp.where(v1 > 0.0, c - pltpu.roll(c, 1, 0), pltpu.roll(c, WY - 1, 0) - c)
        behind = jnp.where(first, 0.0, pltpu.roll(c, 1, 1))
        beyond = jnp.where(last, 0.0, pltpu.roll(c, NZ - 1, 1))
        flow += v2 * jnp.where(v2 > 0.0, c - behind, beyond - c)
        return c - STEP * flow

    sweep_rows(reach, row, dst)


def scatter(src, dst, vw, j, reach):
    first, last = lane_masks((WY, NZ))

    def row(x, xm, xp):
        c = src[x]
        v0, v1, v2 = vw[j, 0, x], vw[j, 1, x], vw[j, 2, x]
        change = (jnp.abs(v0) + jnp.abs(v1) + jnp.abs(v2)) * c
        change -= jnp.maximum(vw[j, 0, xp], 0.0) * src[xp]
        change += jnp.minimum(vw[j, 0, xm], 0.0) * src[xm]
        change -= pltpu.roll(jnp.maximum(v1, 0.0) * c, WY - 1, 0)
        change += pltpu.roll(jnp.minimum(v1, 0.0) * c, 1, 0)
        change -= jnp.where(last, 0.0, pltpu.roll(jnp.maximum(v2, 0.0) * c, NZ - 1, 1))
        change += jnp.where(first, 0.0, pltpu.roll(jnp.minimum(v2, 0.0) * c, 1, 1))
        return c - STEP * change

    sweep_rows(reach, row, dst)


def clear_halo(ref, x_rows=True):
    zero_row = jnp.zeros((WY, NZ), F32)
    for x in range(CX, WX):
        ref[x] = zero_row


def repack(velocity, counts):
    tiles = NY // CY

    def kernel(counts, src, dst, held, note, isem, osem):
        value = jnp.full((CY, NZ), counts[0], jnp.int32).astype(F32)
        note[0] = value
        arrive, leave = [], []
        for c in range(tiles):
            for d in range(3):
                n = c * 3 + d
                copy = pltpu.make_async_copy(src.at[0, d, :, c * CY : (c + 1) * CY], held.at[c, d], isem.at[n])
                copy.start()
                arrive.append(copy)
        for c in range(tiles):
            copy = pltpu.make_async_copy(note, dst.at[c, 3 * CX : VBLOCKS], osem.at[24 + c])
            copy.start()
            leave.append(copy)
            for d in range(3):
                n = c * 3 + d
                arrive[n].wait()
                copy = pltpu.make_async_copy(held.at[c, d], dst.at[c, d * CX : (d + 1) * CX], osem.at[n])
                copy.start()
                leave.append(copy)
        wait_all(leave)

    return pl.pallas_call(
        kernel,
        out_shape=sds(tiles, VBLOCKS, CY, NZ),
        in_specs=[scalars(), anywhere()],
        out_specs=anywhere(),
        scratch_shapes=[
            VMEM((tiles, 3, CX, CY, NZ), F32),
            VMEM((1, CY, NZ), F32),
            pltpu.SemaphoreType.DMA((24,)),
            pltpu.SemaphoreType.DMA((32,)),
        ],
        compiler_params=params(),
    )(counts, velocity)


def template(info, table, atlas, labels):
    def kernel(info, table, atlas, labels, tmpl):
        def one(x, carry):
            lab = labels[x]
            value = jnp.zeros((CY, NZ), F32)
            for l in range(64):
                value = jnp.where(lab == l, table[l], value)
            tmpl[x] = atlas[x] + value
            return carry

        lax.fori_loop(0, CX, one, 0)

    return pl.pallas_call(
        kernel,
        out_shape=sds(CX, CY, NZ),
        in_specs=[scalars(), scalars(), whole(), whole()],
        out_specs=whole(),
        compiler_params=params(),
    )(info, table, atlas, labels)


def image_edges(info, tile, ra, rb):
    def kernel(info, tile, ra, rb, win, ec, ed):
        px, py = info[2], info[3]
        win[0:CX] = tile[...]
        win[pl.ds(jnp.where(px == 0, CX, WX - DEPTH), DEPTH)] = ra[...]
        win[pl.ds(jnp.where(px == 0, WX - DEPTH, CX), DEPTH)] = rb[...]
        sub = rows8()

        def one(i, carry):
            def tile_of(key):
                return win[i + key, 0:8], win[i + key, 8:16]

            top, bottom = pack_edges(((0, 4, 0), (12, 4, 4)), tile_of, sub)
            ec[i] = jnp.where(py == 0, top, bottom)
            ed[i] = jnp.where(py == 0, bottom, top)
            return carry

        lax.fori_loop(0, 12, one, 0)

    return pl.pallas_call(
        kernel,
        out_shape=[sds(WX, CY, NZ), sds(12, 8, NZ), sds(12, 8, NZ)],
        in_specs=[scalars()] + [whole()] * 3,
        out_specs=[whole()] * 3,
        compiler_params=params(),
    )(info, tile, ra, rb)


def faces(info, vt, tile, *before):
    def kernel(info, vt, tile, *refs):
        ea, eb, sem = refs[-3:]
        px = info[2]
        pairs = []
        for g in range(2):
            for d in range(3):
                for j, k, off in V_SLOTS:
                    top = jnp.where(px == 0, CX - k, 0) + d * CX
                    bottom = jnp.where(px == 0, 0, CX - k) + d * CX
                    row = (g * 3 + d) * V_ROWS + off
                    pairs.append((vt.at[4 * g + j, pl.ds(top, k)], ea.at[row : row + k]))
                    pairs.append((vt.at[4 * g + j, pl.ds(bottom, k)], eb.at[row : row + k]))
        started = copies(pairs, sem)
        ea[FACE : FACE + DEPTH] = tile[pl.ds(jnp.where(px == 0, CX - DEPTH, 0), DEPTH)]
        eb[FACE : FACE + DEPTH] = tile[pl.ds(jnp.where(px == 0, 0, CX - DEPTH), DEPTH)]
        wait_all(started)

    return pl.pallas_call(
        kernel,
        out_shape=[sds(FACE + DEPTH, CY, NZ)] * 2,
        in_specs=[scalars(), anywhere(), whole()] + [anywhere()] * len(before),
        out_specs=[whole()] * 2,
        scratch_shapes=[pltpu.SemaphoreType.DMA((36,))],
        compiler_params=params(),
    )(info, vt, tile, *before)


def velocity_edges(info, vt, ra, rb, group, tile=None):
    with_image = tile is not None
    rows = VX + 4 if with_image else VX

    def kernel(info, vt, ra, rb, va, vb, *refs):
        ec, ed = refs[-2:]
        px, py = info[2], info[3]
        sub = rows8()

        def emit(i, slots, tile_of):
            top, bottom = pack_edges(slots, tile_of, sub)
            ec[0, i] = jnp.where(py == 0, top, bottom)
            ed[0, i] = jnp.where(py == 0, bottom, top)

        def one(i, carry):
            for r in range(2):
                x = 2 * i + r
                emit(x, V_SLOTS, lambda j: (vt[j, x, 0:8], vt[j, x, 8:16]))
            return carry

        lax.fori_loop(0, CX // 2, one, 0)
        for i in range(3):
            up, down = [], []
            for j, k, off in V_SLOTS:
                if i < k:
                    up.append((j, k, off))
                if i >= 3 - k:
                    down.append((j, k, off))

            def halves(value):
                return value[0:8], value[8:16]

            def tile_up(j):
                row = V_SLOTS[j][2] + i
                return halves(jnp.where(px == 0, ra[row], rb[row]))

            def tile_down(j):
                row = V_SLOTS[j][2] + i - (3 - V_SLOTS[j][1])
                return halves(jnp.where(px == 0, rb[row], ra[row]))

            emit(CX + i, up, tile_up)
            emit(CX + 3 + i, down, tile_down)
        if with_image:
            own = refs[0]
            d = pl.program_id(0)
            for i in range(4):
                other = jnp.where(px == d - 1, va[i], vb[i])
                other = jnp.where(d == 0, own[12 + i], other)
                near = own[4 * d + i]
                pair = ((near[0:8], near[8:16]), (other[0:8], other[8:16]))
                emit(VX + i, ((0, 4, 0), (1, 4, 4)), lambda key: pair[key])

    image_face = pl.BlockSpec((DEPTH, CY, NZ), lambda d: (FACE // DEPTH, 0, 0))
    face = pl.BlockSpec((V_ROWS, CY, NZ), lambda d: (group * 3 + d, 0, 0))
    return pl.pallas_call(
        kernel,
        grid=(3,),
        out_shape=[sds(3, rows, 8, NZ)] * 2,
        in_specs=[
            scalars(),
            pl.BlockSpec((4, CX, CY, NZ), lambda d: (group, d, 0, 0)),
            face,
            face,
            image_face,
            image_face,
        ]
        + ([pl.BlockSpec((CX, CY, NZ), lambda d: (0, 0, 0))] if with_image else []),
        out_specs=[pl.BlockSpec((1, rows, 8, NZ), lambda d: (d, 0, 0, 0))] * 2,
        compiler_params=params(),
    )(info, vt, ra, rb, ra, rb, *((tile,) if with_image else ()))


def forward_first(info, tile, vt, ra, rb, yc, yd, *before):
    def kernel(info, tile, vt, ra, rb, yc, yd, *refs):
        pack, ea, eb, i4, vw, image, halos, hsem, sem, osem = refs[len(before) :]
        px, py = info[2], info[3]
        pair = copies([(ra.at[FACE : FACE + DEPTH], halos.at[0]), (rb.at[FACE : FACE + DEPTH], halos.at[1])], hsem)
        started = fill_velocity(0, info, vt, ra, rb, yc, yd, vw, sem)
        image[0, 0:CX, 0:CY] = tile[...]
        wait_all(pair)
        image[0, pl.ds(jnp.where(px == 0, CX, WX - DEPTH), DEPTH), 0:CY] = halos[0]
        image[0, pl.ds(jnp.where(px == 0, WX - DEPTH, CX), DEPTH), 0:CY] = halos[1]
        sub = rows8()
        for j in range(12):
            c, e = yc[j // 4, VX + j % 4], yd[j // 4, VX + j % 4]
            above = jnp.where(py == 0, c, e)
            below = jnp.where(py == 0, e, c)
            image[0, j, CY:WY] = halo_block(above, below, 4, 0, sub)
            image[0, j + 12, CY:WY] = halo_block(above, below, 4, 4, sub)
        wait_all(started)
        out = []
        for j in range(4):
            advance(image.at[j], image.at[j + 1], vw, j, 3 - j)
            out.append(pltpu.make_async_copy(image.at[j, 0:CX, 0:CY], pack.at[j, 0], osem.at[j]))
            out[-1].start()
        last = image.at[4]
        i4[...] = last[0:CX, 0:CY]
        ea[...] = last[pl.ds(jnp.where(px == 0, CX - DEPTH, 0), DEPTH), 0:CY]
        eb[...] = last[pl.ds(jnp.where(px == 0, 0, CX - DEPTH), DEPTH), 0:CY]
        wait_all(out)

    return pl.pallas_call(
        kernel,
        out_shape=[
            sds(NT, 2, CX, CY, NZ),
            sds(DEPTH, CY, NZ),
            sds(DEPTH, CY, NZ),
            sds(CX, CY, NZ),
            sds(4, 3, WX, WY, NZ),
        ],
        in_specs=[scalars(), whole()] + [anywhere()] * 3 + [whole()] * 2 + [anywhere()] * len(before),
        out_specs=[anywhere()] + [whole()] * 4,
        scratch_shapes=[
            VMEM((5, WX, WY, NZ), F32),
            VMEM((2, DEPTH, CY, NZ), F32),
            pltpu.SemaphoreType.DMA((2,)),
            pltpu.SemaphoreType.DMA((FILL_COPIES,)),
            pltpu.SemaphoreType.DMA((4,)),
        ],
        compiler_params=params(),
    )(info, tile, vt, ra, rb, yc, yd, *before)


def window(info, vt, ra, rb, yc, yd, group):
    def kernel(info, vt, ra, rb, yc, yd, vw, sem):
        wait_all(fill_velocity(group, info, vt, ra, rb, yc, yd, vw, sem))

    return pl.pallas_call(
        kernel,
        out_shape=sds(4, 3, WX, WY, NZ),
        in_specs=[scalars()] + [anywhere()] * 3 + [whole()] * 2,
        out_specs=whole(),
        scratch_shapes=[pltpu.SemaphoreType.DMA((FILL_COPIES,))],
        compiler_params=params(),
    )(info, vt, ra, rb, yc, yd)


def send_rows(info, widths, source, ea, eb):
    px = info[2]
    off = 0
    for n, k in enumerate(widths):
        top = jnp.where(px == 0, CX, WX - k)
        bottom = jnp.where(px == 0, WX - k, CX)
        ea[off : off + k] = source(n)[pl.ds(top, k)]
        eb[off : off + k] = source(n)[pl.ds(bottom, k)]
        off += k


MID_WIDTHS = (4, 3, 2, 1)
MID_SLOTS = ((0, 4, 0), (1, 3, 4), (3, 1, 7))
END_WIDTHS = (3, 2, 1)
END_SLOTS = ((0, 3, 0), (1, 2, 3), (2, 1, 5), (3, 2, 6))


def forward_second(info, win, ic, idd, target, vw, pack, *before):
    def kernel(info, win, ic, idd, target, vw, pack_in, *refs):
        pack, lw, ea, eb, image, lam, osem = refs[len(before) :]
        fill_image(info, win, ic, idd, image.at[0])
        for n in range(4):
            clear_halo(lam.at[n])
        out = []
        for j in range(4):
            advance(image.at[j], image.at[j + 1], vw, j, 3 - j)
            out.append(pltpu.make_async_copy(image.at[j, 0:CX, 0:CY], pack.at[4 + j, 0], osem.at[j]))
            out[-1].start()
        count = info[4]
        inside = lax.broadcasted_iota(jnp.int32, (CY, NZ), 0) * NZ + lax.broadcasted_iota(jnp.int32, (CY, NZ), 1)
        zero = jnp.zeros((8, NZ), F32)

        def one(x, carry):
            value = image[4, x, 0:CY] - target[x]
            lam[0, x, 0:CY] = jnp.where(inside + x * (CY * NZ) < count, value, 0.0)
            lam[0, x, CY:WY] = zero
            return carry

        lax.fori_loop(0, CX, one, 0)
        out.append(pltpu.make_async_copy(lam.at[0, 0:CX, 0:CY], pack.at[7, 1], osem.at[4]))
        out[-1].start()
        for n in range(4):
            scatter(lam.at[n], lam.at[n + 1], vw, 3 - n, n + 1)
        for n in range(4):
            lw[n] = lam[4 - n, 0:CX]
        send_rows(info, MID_WIDTHS, lambda n: lam.at[4 - n], ea, eb)
        wait_all(out)

    return pl.pallas_call(
        kernel,
        out_shape=[sds(NT, 2, CX, CY, NZ), sds(4, CX, WY, NZ), sds(10, WY, NZ), sds(10, WY, NZ)],
        in_specs=[scalars()] + [whole()] * 5 + [anywhere()] * (1 + len(before)),
        out_specs=[anywhere()] + [whole()] * 3,
        scratch_shapes=[
            VMEM((5, WX, WY, NZ), F32),
            VMEM((5, WX, WY, NZ), F32),
            pltpu.SemaphoreType.DMA((5,)),
        ],
        input_output_aliases={6: 0},
        compiler_params=params(),
    )(info, win, ic, idd, target, vw, pack, *before)


def costate_edges(info, lw, ra, rb, widths, slots):
    def kernel(info, lw_in, ra, rb, lw, ec, ed):
        px, py = info[2], info[3]
        off = 0
        for n, k in enumerate(widths):
            for i in range(k):
                to_a = jnp.where(px == 0, CX - k, 0) + i
                to_b = jnp.where(px == 0, 0, CX - k) + i
                lw[n, to_a] = lw[n, to_a] + ra[off + i]
                lw[n, to_b] = lw[n, to_b] + rb[off + i]
            off += k
        sub = rows8()

        def one(x, carry):
            top = jnp.zeros((8, NZ), F32)
            bottom = top
            for n, k, off in slots:
                block = lw[n, x, CY:WY]
                top = put(top, block, off, off, off + k, sub)
                bottom = put(bottom, block, off + k, off, off + k, sub)
            ec[x] = jnp.where(py == 0, top, bottom)
            ed[x] = jnp.where(py == 0, bottom, top)
            return carry

        lax.fori_loop(0, CX, one, 0)

    return pl.pallas_call(
        kernel,
        out_shape=[sds(4, CX, WY, NZ), sds(CX, 8, NZ), sds(CX, 8, NZ)],
        in_specs=[scalars()] + [whole()] * 3,
        out_specs=[whole()] * 3,
        input_output_aliases={1: 0},
        compiler_params=params(),
    )(info, lw, ra, rb)


def take(c, e, py, k, off, sub):
    below = jnp.where(py == 0, e, c)
    above = jnp.where(py == 0, c, e)
    zero = jnp.zeros((8, NZ), F32)
    return put(zero, below, -off, 0, k, sub), put(zero, above, 8 - k - off, 8 - k, 8, sub)


def backward_second(info, lw, lc, ld, vw, pack, *before):
    def kernel(info, lw, lc, ld, vw, pack_in, *refs):
        pack, lw2, ea, eb, lam, done, osem = refs[len(before) :]
        for n in range(3):
            clear_halo(lam.at[n])
        py = info[3]
        sub = rows8()
        zero = jnp.zeros((8, NZ), F32)

        def one(x, carry):
            c, e = lc[x], ld[x]
            for n, k, off in MID_SLOTS:
                low, high = take(c, e, py, k, off, sub)
                low, high = lw[n, x, 0:8] + low, lw[n, x, 8:16] + high
                if n == 0:
                    lam[0, x, 0:8] = low
                    lam[0, x, 8:16] = high
                    lam[0, x, CY:WY] = zero
                else:
                    done[(n - 1) // 2, x, 0:8] = low
                    done[(n - 1) // 2, x, 8:16] = high
            return carry

        lax.fori_loop(0, CX, one, 0)
        out = [
            pltpu.make_async_copy(lam.at[0, 0:CX, 0:CY], pack.at[3, 1], osem.at[0]),
            pltpu.make_async_copy(done.at[0], pack.at[4, 1], osem.at[1]),
            pltpu.make_async_copy(done.at[1], pack.at[6, 1], osem.at[2]),
        ]
        for copy in out:
            copy.start()
        for n in range(3):
            scatter(lam.at[n], lam.at[n + 1], vw, 3 - n, n + 1)
        for n in range(3):
            lw2[n] = lam[3 - n, 0:CX]
        lw2[3] = lw[2]
        send_rows(info, END_WIDTHS, lambda n: lam.at[3 - n], ea, eb)
        wait_all(out)

    return pl.pallas_call(
        kernel,
        out_shape=[sds(NT, 2, CX, CY, NZ), sds(4, CX, WY, NZ), sds(6, WY, NZ), sds(6, WY, NZ)],
        in_specs=[scalars()] + [whole()] * 4 + [anywhere()] * (1 + len(before)),
        out_specs=[anywhere()] + [whole()] * 3,
        scratch_shapes=[
            VMEM((4, WX, WY, NZ), F32),
            VMEM((2, CX, CY, NZ), F32),
            pltpu.SemaphoreType.DMA((3,)),
        ],
        input_output_aliases={5: 0},
        compiler_params=params(),
    )(info, lw, lc, ld, vw, pack, *before)


def costate_finish(info, lw, lc, ld, pack, *before):
    def kernel(info, lw, lc, ld, pack_in, *refs):
        pack, done, sem = refs[len(before) :]
        py = info[3]
        sub = rows8()

        def one(x, carry):
            c, e = lc[x], ld[x]
            for n, k, off in END_SLOTS:
                low, high = take(c, e, py, k, off, sub)
                done[n, x, 0:8] = lw[n, x, 0:8] + low
                done[n, x, 8:16] = lw[n, x, 8:16] + high
            return carry

        lax.fori_loop(0, CX, one, 0)
        wait_all(copies([(done.at[n], pack.at[m, 1]) for n, m in enumerate((0, 1, 2, 5))], sem))

    return pl.pallas_call(
        kernel,
        out_shape=sds(NT, 2, CX, CY, NZ),
        in_specs=[scalars()] + [whole()] * 3 + [anywhere()] * (1 + len(before)),
        out_specs=anywhere(),
        scratch_shapes=[VMEM((4, CX, CY, NZ), F32), pltpu.SemaphoreType.DMA((4,))],
        input_output_aliases={4: 0},
        compiler_params=params(),
    )(info, lw, lc, ld, pack, *before)


def masks(shape):
    first, last = lane_masks(shape)
    y = lax.broadcasted_iota(jnp.int32, shape, 0)
    return first, last, y == 0, y == NY - 1


def shifted(c, m):
    first, last, bottom, top = m
    return (
        jnp.where(bottom, 0.0, pltpu.roll(c, 1, 0)),
        jnp.where(top, 0.0, pltpu.roll(c, NY - 1, 0)),
        jnp.where(first, 0.0, pltpu.roll(c, 1, 1)),
        jnp.where(last, 0.0, pltpu.roll(c, NZ - 1, 1)),
    )


def smooth(before, c, after, m):
    near = before + after
    for value in shifted(c, m):
        near += value
    return c + KAPPA * (near - 6.0 * c)


def slope(v, before, c, after, direction, m):
    if direction == 0:
        return jnp.where(v > 0.0, c - before, after - c)
    first, last, bottom, top = m
    axis, size, low, high = (0, NY, bottom, top) if direction == 1 else (1, NZ, first, last)
    behind = jnp.where(low, 0.0, pltpu.roll(c, 1, axis))
    beyond = jnp.where(high, 0.0, pltpu.roll(c, size - 1, axis))
    return jnp.where(v > 0.0, c - behind, beyond - c)


def finish_inside(weight, velocity, pack):
    def kernel(weight, vel, pack, out, keep_c, keep_s, islab, lslab, grad, soft, sem):
        d = pl.program_id(0)
        coef = weight[0]

        @pl.when(d == 0)
        def _():
            pairs = []
            for c in range(NY // CY):
                y = slice(c * CY, (c + 1) * CY)
                pairs += [(pack.at[c, 0], islab.at[:, y]), (pack.at[c, 1], lslab.at[:, y])]
            wait_all(copies(pairs, sem))

        m = masks((NY, NZ))
        for direction in range(3):

            @pl.when(d == direction)
            def _(direction=direction):
                def one(x, carry):
                    g = slope(vel[0, 0, x], islab[x - 1], islab[x], islab[x + 1], direction, m)
                    grad[x] = (coef * lslab[x]) * g
                    return carry

                lax.fori_loop(1, CX - 1, one, 0)

        def once(x, carry):
            soft[x] = smooth(grad[x - 1], grad[x], grad[x + 1], m)
            return carry

        lax.fori_loop(2, CX - 2, once, 0)

        def twice(x, carry):
            out[0, 0, x] = vel[0, 0, x] + smooth(soft[x - 1], soft[x], soft[x + 1], m)
            return carry

        lax.fori_loop(3, CX - 3, twice, 0)
        for n, (x, y) in enumerate(((1, 2), (2, 3), (13, 12), (14, 13))):
            keep_c[0, n] = grad[x]
            keep_s[0, n] = soft[y]

    slab = pl.BlockSpec((1, 1, CX, NY, NZ), lambda d: (0, d, 0, 0, 0))
    kept = pl.BlockSpec((1, 4, NY, NZ), lambda d: (d, 0, 0, 0))
    return pl.pallas_call(
        kernel,
        grid=(3,),
        out_shape=[sds(1, 3, CX, NY, NZ), sds(3, 4, NY, NZ), sds(3, 4, NY, NZ)],
        in_specs=[scalars(), slab, anywhere()],
        out_specs=[slab, kept, kept],
        scratch_shapes=[VMEM((CX, NY, NZ), F32)] * 4 + [pltpu.SemaphoreType.DMA((16,))],
        compiler_params=params(),
    )(weight, velocity, pack)


def finish_edges(info, weight, velocity, va, vb, pack, fa, fb, keep_c, keep_s, partial):
    def kernel(info, weight, vel, va, vb, pack, fa, fb, keep_c, keep_s, partial, out, slabs, vrows, grad, soft, result, sem, vsem, osem):
        d = pl.program_id(0)
        px = info[2]
        coef = weight[0]

        @pl.when(d == 0)
        def _():
            pairs = []
            above, below = jnp.where(px == 0, 1, 0), jnp.where(px == 0, 0, 1)
            hi, hl = jnp.where(px == 0, 2, 0), jnp.where(px == 0, 6, 5)
            bi, bl = jnp.where(px == 0, 0, 2), jnp.where(px == 0, 5, 6)
            for c in range(NY // CY):
                y = slice(c * CY, (c + 1) * CY)
                pairs += [
                    (pack.at[c, 0, 0:2], slabs.at[0, 3:5, y]),
                    (pack.at[c, 1, 0:1], slabs.at[0, 7:8, y]),
                    (pack.at[c, 0, CX - 2 : CX], slabs.at[1, 0:2, y]),
                    (pack.at[c, 1, CX - 1 : CX], slabs.at[1, 5:6, y]),
                    (fa.at[c, 0:3], slabs.at[above, pl.ds(hi, 3), y]),
                    (fa.at[c, 3:5], slabs.at[above, pl.ds(hl, 2), y]),
                    (fb.at[c, 0:3], slabs.at[below, pl.ds(bi, 3), y]),
                    (fb.at[c, 3:5], slabs.at[below, pl.ds(bl, 2), y]),
                ]
            wait_all(copies(pairs, sem))

        wait_all(
            copies([(vel.at[0, d, 0:3], vrows.at[0]), (vel.at[0, d, CX - 3 : CX], vrows.at[1])], vsem)
        )
        m = masks((NY, NZ))
        for direction in range(3):

            @pl.when(d == direction)
            def _(direction=direction):
                for side in range(2):
                    for n in range(3):
                        own = n == 2 if side == 0 else n == 0
                        if own:
                            v = vrows[0, 0] if side == 0 else vrows[1, 2]
                        else:
                            k = n if side == 0 else n - 1
                            v = jnp.where((px == 0) == (side == 1), va[0, k], vb[0, k])
                        g = slope(v, slabs[side, n], slabs[side, n + 1], slabs[side, n + 2], direction, m)
                        grad[side, n] = (coef * slabs[side, 5 + n]) * g

        for n in range(2):
            grad[0, 3 + n] = keep_c[0, n]
            grad[1, 3 + n] = keep_c[0, 2 + n]
        zero = jnp.zeros((NY, NZ), F32)
        for side in range(2):
            order = [0, 1, 2, 3, 4] if side == 0 else [3, 4, 0, 1, 2]
            for n in range(3):
                soft[side, n] = smooth(grad[side, order[n]], grad[side, order[n + 1]], grad[side, order[n + 2]], m)

        @pl.when(info[0] == 0)
        def _():
            soft[0, 0] = zero

        @pl.when(info[0] == info[5] - 1)
        def _():
            soft[1, 2] = zero

        low = [soft.at[0, 0], soft.at[0, 1], soft.at[0, 2], keep_s.at[0, 0], keep_s.at[0, 1]]
        high = [keep_s.at[0, 2], keep_s.at[0, 3], soft.at[1, 0], soft.at[1, 1], soft.at[1, 2]]
        for side, rows in enumerate((low, high)):
            for n in range(3):
                result[side, n] = vrows[side, n] + smooth(rows[n][...], rows[n + 1][...], rows[n + 2][...], m)
        wait_all(
            copies([(result.at[0], out.at[0, d, 0:3]), (result.at[1], out.at[0, d, CX - 3 : CX])], osem)
        )

    face = pl.BlockSpec((1, 2, NY, NZ), lambda d: (d, 0, 0, 0))
    kept = pl.BlockSpec((1, 4, NY, NZ), lambda d: (d, 0, 0, 0))
    return pl.pallas_call(
        kernel,
        grid=(3,),
        out_shape=sds(1, 3, CX, NY, NZ),
        in_specs=[scalars(), scalars(), anywhere(), face, face] + [anywhere()] * 3 + [kept, kept, anywhere()],
        out_specs=anywhere(),
        scratch_shapes=[
            VMEM((2, 8, NY, NZ), F32),
            VMEM((2, 3, NY, NZ), F32),
            VMEM((2, 5, NY, NZ), F32),
            VMEM((2, 3, NY, NZ), F32),
            VMEM((2, 3, NY, NZ), F32),
            pltpu.SemaphoreType.DMA((64,)),
            pltpu.SemaphoreType.DMA((2,)),
            pltpu.SemaphoreType.DMA((2,)),
        ],
        input_output_aliases={10: 0},
        compiler_params=params(),
    )(info, weight, velocity, va, vb, pack, fa, fb, keep_c, keep_s, partial)


def edge_rows(value, dim, k, px):
    length = value.shape[dim]
    high = lax.slice_in_dim(value, length - k, length, axis=dim)
    low = lax.slice_in_dim(value, 0, k, axis=dim)
    return jnp.where(px == 0, high, low), jnp.where(px == 0, low, high)


def shards(velocity, atlas_image, target, labels, label_table, counts):
    s, c = lax.axis_index("space"), lax.axis_index("cuts")
    px, py = s % 2, c % 2
    info = jnp.stack([s, c, px, py, counts[0], jnp.int32(lax.axis_size("space")), s, s]).astype(jnp.int32)
    vt = lax.all_to_all(repack(velocity, counts), "cuts", split_axis=0, concat_axis=0, tiled=True)

    tile = template(info, label_table, atlas_image, labels)
    ova, ovb = edge_rows(velocity[0], 1, 2, px)
    ova, ovb = swap(ova, ovb, "space")

    fa, fb = swap(*faces(info, vt, tile, ova, ovb), "space")
    total = jnp.broadcast_to(jnp.sum(vt[:, 3 * CX, 0, 0]), (1, 128))
    y0 = swap(*velocity_edges(info, vt, fa, fb, 0, tile), "cuts")
    y1 = swap(*velocity_edges(info, vt, fa, fb, 1), "cuts")
    pack, ea, eb, i4, vw0 = forward_first(info, tile, vt, fa, fb, *y0)
    total = xor_swap(total, 1)
    win, ec, ed = image_edges(info, i4, *swap(ea, eb, "space"))
    vw1 = window(info, vt, fa, fb, *y1, 1)
    ic, idd = swap(ec, ed, "cuts")
    pack, lw, ea, eb = forward_second(info, win, ic, idd, target, vw1, pack, total)
    total = xor_swap(total, 2)
    lw, ec, ed = costate_edges(info, lw, *swap(ea, eb, "space"), MID_WIDTHS, MID_SLOTS)
    ec, ed = swap(ec, ed, "cuts")
    pack, lw, ea, eb = backward_second(info, lw, ec, ed, vw0, pack, total)
    total = xor_swap(total, 4)
    lw, ec, ed = costate_edges(info, lw, *swap(ea, eb, "space"), END_WIDTHS, END_SLOTS)
    ec, ed = swap(ec, ed, "cuts")
    pack = costate_finish(info, lw, ec, ed, pack, total)
    total = xor_swap(total, 8)
    pack = lax.all_to_all(pack, "cuts", split_axis=0, concat_axis=0, tiled=True)

    cells = CX * CY * NZ * lax.axis_size("space") * lax.axis_size("cuts")
    weight = jnp.reshape(-STEP * DATA_WEIGHT * (cells / total[0, 0]), (1,)).astype(F32)
    rows = [jnp.concatenate([pack[:, 0, a : a + 3], pack[:, 1, b : b + 2]], axis=1) for a, b in ((CX - 3, CX - 2), (0, 0))]
    ea, eb = jnp.where(px == 0, rows[0], rows[1]), jnp.where(px == 0, rows[1], rows[0])
    fa, fb = swap(ea, eb, "space")
    partial, keep_c, keep_s = finish_inside(weight, velocity, pack)
    return finish_edges(info, weight, velocity, ova, ovb, pack, fa, fb, keep_c, keep_s, partial)


def solution(mesh):
    in_specs = (
        P("cuts", None, "space", None, None),
        P("space", "cuts", None),
        P("space", "cuts", None),
        P("space", "cuts", None),
        P(),
        P(("space", "cuts")),
    )
    out_specs = P("cuts", None, "space", None, None)
    return jax.shard_map(shards, mesh=mesh, in_specs=in_specs, out_specs=out_specs, check_vma=False)
```

```python
import functools

import jax
import jax.numpy as jnp
from jax import lax
from jax.experimental import pallas as pl
from jax.experimental.pallas import tpu as pltpu
from jax.sharding import PartitionSpec as P

F32 = jnp.float32
NT = 8
STEP = 1.0 / NT
DATA_WEIGHT = 4.0
KAPPA = 0.125
CX, CY, NZ = 16, 16, 256
NY = 128
DEPTH = 4
WX, WY = CX + 2 * DEPTH, CY + 2 * DEPTH
V_SLOTS = ((0, 3, 0), (1, 2, 3), (2, 1, 5))
V_ROWS = 6
VX = CX + 6
VBLOCKS = 3 * CX
PBLOCKS = 2 * CX + 1
HALF = VBLOCKS // 2
RING = 4
FACE = 3 * V_ROWS
VMEM = pltpu.VMEM
ANY = pl.ANY


def whole():
    return pl.BlockSpec(memory_space=VMEM)


def anywhere():
    return pl.BlockSpec(memory_space=ANY)


def hbm():
    return pl.BlockSpec(memory_space=pltpu.HBM)


def scalars():
    return pl.BlockSpec(memory_space=pltpu.SMEM)


def params(mib=16):
    return pltpu.CompilerParams(vmem_limit_bytes=mib * 1024 * 1024)


def sds(*shape):
    return jax.ShapeDtypeStruct(shape, F32)


def swaps(size, first):
    pairs = []
    for i in range(first, size - 1, 2):
        pairs += [(i, i + 1), (i + 1, i)]
    return pairs


def swap(even, odd, axis):
    size = lax.axis_size(axis)
    return lax.ppermute(even, axis, swaps(size, 0)), lax.ppermute(odd, axis, swaps(size, 1))


def xor_swap(value, reach):
    size = lax.axis_size("space")
    return value + lax.ppermute(value, "space", [(i, i ^ reach) for i in range(size)])


def rows8():
    return lax.broadcasted_iota(jnp.int32, (8, NZ), 0)


def turn(block, shift):
    shift = shift % 8
    return pltpu.roll(block, shift, 0) if shift else block


def put(total, block, shift, low, high, sub):
    return jnp.where((sub >= low) & (sub < high), turn(block, shift), total)


def pack_edges(slots, tile, sub):
    top = jnp.zeros((8, NZ), F32)
    bottom = top
    for key, k, off in slots:
        low8, high8 = tile(key)
        top = put(top, high8, off + k, off, off + k, sub)
        bottom = put(bottom, low8, off, off, off + k, sub)
    return top, bottom


def halo_block(above, below, k, off, sub):
    block = put(jnp.zeros((8, NZ), F32), above, -off, 0, k, sub)
    return put(block, below, 8 - k - off, 8 - k, 8, sub)


def lane_masks(shape):
    z = lax.broadcasted_iota(jnp.int32, shape, 1)
    return z == 0, z == NZ - 1


def copies(pairs, sem):
    started = [pltpu.make_async_copy(a, b, sem.at[i]) for i, (a, b) in enumerate(pairs)]
    for copy in started:
        copy.start()
    return started


def wait_all(started):
    for copy in started:
        copy.wait()


def fill_velocity(group, info, vt, ra, rb, yc, yd, vw, sem):
    px, py = info[2], info[3]
    pairs = []
    for d in range(3):
        for j in range(4):
            pairs.append((vt.at[4 * group + j, d * CX : (d + 1) * CX], vw.at[j, d, 0:CX, 0:CY]))
        for j, k, off in V_SLOTS:
            to_a = jnp.where(px == 0, CX, WX - k)
            to_b = jnp.where(px == 0, WX - k, CX)
            row = d * V_ROWS + off
            pairs.append((ra.at[row : row + k], vw.at[j, d, pl.ds(to_a, k), 0:CY]))
            pairs.append((rb.at[row : row + k], vw.at[j, d, pl.ds(to_b, k), 0:CY]))
    started = copies(pairs, sem)
    sub = rows8()
    zero_row = jnp.zeros((WY, NZ), F32)
    zero_tile = jnp.zeros((8, NZ), F32)
    for j in range(4):
        k = 3 - j
        for d in range(3):
            for x in range(CX + k, WX - k):
                vw[j, d, x] = zero_row

    def blocks(d, i, x, keep):
        c, e = yc[d, i], yd[d, i]
        above = jnp.where(py == 0, c, e)
        below = jnp.where(py == 0, e, c)
        for j, k, off in V_SLOTS:
            if keep(k):
                vw[j, d, x, CY:WY] = halo_block(above, below, k, off, sub)

    def one(i, carry):
        for d in range(3):
            for r in range(2):
                blocks(d, 2 * i + r, 2 * i + r, lambda k: True)
                vw[3, d, 2 * i + r, CY:WY] = zero_tile
        return carry

    lax.fori_loop(0, CX // 2, one, 0)
    for i in range(CX, VX):
        x = i if i < CX + 3 else i + 2
        for d in range(3):
            blocks(d, i, x, lambda k: x < CX + k or x >= WX - k)
    return started


FILL_COPIES = 30


def fill_image(info, win, yc, yd, image):
    py = info[3]
    sub = rows8()

    def one(i, carry):
        c, e = yc[i], yd[i]
        above = jnp.where(py == 0, c, e)
        below = jnp.where(py == 0, e, c)
        image[i, 0:CY] = win[i]
        image[i + 12, 0:CY] = win[i + 12]
        image[i, CY:WY] = halo_block(above, below, 4, 0, sub)
        image[i + 12, CY:WY] = halo_block(above, below, 4, 4, sub)
        return carry

    lax.fori_loop(0, 12, one, 0)


ROWS = 2


def sweep_rows(reach, row, dst):
    turns = -(-(CX + 2 * reach) // ROWS)

    def one(i, carry):
        xs = [lax.rem(i * ROWS + r - reach + WX, WX) for r in range(ROWS)]
        values = [row(x, lax.rem(x + WX - 1, WX), lax.rem(x + 1, WX)) for x in xs]
        for x, value in zip(xs, values):
            dst[x] = value
        return carry

    lax.fori_loop(0, turns, one, 0)


def advance(src, dst, vw, j, reach):
    first, last = lane_masks((WY, NZ))

    def row(x, xm, xp):
        c = src[x]
        v0, v1, v2 = vw[j, 0, x], vw[j, 1, x], vw[j, 2, x]
        flow = v0 * jnp.where(v0 > 0.0, c - src[xm], src[xp] - c)
        flow += v1 * jnp.where(v1 > 0.0, c - pltpu.roll(c, 1, 0), pltpu.roll(c, WY - 1, 0) - c)
        behind = jnp.where(first, 0.0, pltpu.roll(c, 1, 1))
        beyond = jnp.where(last, 0.0, pltpu.roll(c, NZ - 1, 1))
        flow += v2 * jnp.where(v2 > 0.0, c - behind, beyond - c)
        return c - STEP * flow

    sweep_rows(reach, row, dst)


def scatter(src, dst, vw, j, reach):
    first, last = lane_masks((WY, NZ))

    def row(x, xm, xp):
        c = src[x]
        v0, v1, v2 = vw[j, 0, x], vw[j, 1, x], vw[j, 2, x]
        change = (jnp.abs(v0) + jnp.abs(v1) + jnp.abs(v2)) * c
        change -= jnp.maximum(vw[j, 0, xp], 0.0) * src[xp]
        change += jnp.minimum(vw[j, 0, xm], 0.0) * src[xm]
        change -= pltpu.roll(jnp.maximum(v1, 0.0) * c, WY - 1, 0)
        change += pltpu.roll(jnp.minimum(v1, 0.0) * c, 1, 0)
        change -= jnp.where(last, 0.0, pltpu.roll(jnp.maximum(v2, 0.0) * c, NZ - 1, 1))
        change += jnp.where(first, 0.0, pltpu.roll(jnp.minimum(v2, 0.0) * c, 1, 1))
        return c - STEP * change

    sweep_rows(reach, row, dst)


def clear_halo(ref, x_rows=True):
    zero_row = jnp.zeros((WY, NZ), F32)
    for x in range(CX, WX):
        ref[x] = zero_row


def ring_pairs(up, across, size):
    pairs = []
    for i in range(size):
        ring, at = divmod(i, RING)
        pairs.append((i, ((ring + across) % 2) * RING + (at + up) % RING))
    return pairs


def shift(value, up, across):
    return lax.ppermute(value, "cuts", ring_pairs(up, across, lax.axis_size("cuts")))


DIRECT = ((1, 1), (-1, 1), (0, 1), (1, 0), (-1, 0))


def repack(info, velocity):
    def kernel(info, src, far_a, far_b, *refs):
        direct, own = refs[:5], refs[5]
        held, isem, osem = refs[6:]
        ring, at = lax.div(info[1], RING), lax.rem(info[1], RING)

        def start_in(n, up, across):
            c = lax.rem(ring + across, 2) * RING + lax.rem(at + up + RING, RING)
            rows = pl.ds(pl.multiple_of(c * CY, CY), CY)
            for d in range(3):
                copy = pltpu.make_async_copy(src.at[0, d, :, rows], held.at[n, d * CX : (d + 1) * CX], isem.at[n * 3 + d])
                copy.start()
                arrive[n].append(copy)

        order = ((2, 0), (2, 1)) + DIRECT + ((0, 0),)
        arrive = [[] for _ in order]
        for n, (up, across) in enumerate(order):
            start_in(n, up, across)
        leave = []
        for n in range(8):
            wait_all(arrive[n])
            if n < 2:
                pairs = [(held.at[n, 0:HALF], far_a.at[n]), (held.at[n, HALF:VBLOCKS], far_b.at[n])]
            else:
                pairs = [(held.at[n], direct[n - 2] if n < 7 else own)]
            for source, target in pairs:
                copy = pltpu.make_async_copy(source, target, osem.at[len(leave)])
                copy.start()
                leave.append(copy)
        wait_all(leave)

    return pl.pallas_call(
        kernel,
        out_shape=[sds(2, HALF, CY, NZ)] * 2 + [sds(VBLOCKS, CY, NZ)] * 6,
        in_specs=[scalars(), hbm()],
        out_specs=[anywhere()] * 8,
        scratch_shapes=[
            VMEM((8, VBLOCKS, CY, NZ), F32),
            pltpu.SemaphoreType.DMA((24,)),
            pltpu.SemaphoreType.DMA((10,)),
        ],
        compiler_params=params(60),
    )(info, velocity)


def spread(far_a, far_b, direct):
    far_a, far_b = shift(far_a, 1, 0), shift(far_b, -1, 0)
    got = [shift(block, up, across) for block, (up, across) in zip(direct, DIRECT)]
    a = [shift(far_a[n], 1, n) for n in range(2)]
    b = [shift(far_b[n], -1, n) for n in range(2)]
    return got + a + b, far_a


def origins(info):
    ring, at = lax.div(info[1], RING), lax.rem(info[1], RING)
    moves = DIRECT + ((2, 0), (2, 1), (2, 0), (2, 1))
    return [lax.rem(ring + across, 2) * RING + lax.rem(at - up + RING, RING) for up, across in moves]


def template(info, table, atlas, labels, velocity, *before):
    def kernel(info, table, atlas, labels, velocity, *refs):
        tmpl, ea, eb, sem = refs[len(before) :]
        px = info[2]
        top, bottom = jnp.where(px == 0, CX - 2, 0), jnp.where(px == 0, 0, CX - 2)
        started = copies([(velocity.at[0, :, pl.ds(top, 2)], ea), (velocity.at[0, :, pl.ds(bottom, 2)], eb)], sem)

        def one(x, carry):
            lab = labels[x]
            value = jnp.zeros((CY, NZ), F32)
            for l in range(64):
                value = jnp.where(lab == l, table[l], value)
            tmpl[x] = atlas[x] + value
            return carry

        lax.fori_loop(0, CX, one, 0)
        wait_all(started)

    return pl.pallas_call(
        kernel,
        out_shape=[sds(CX, CY, NZ), sds(3, 2, NY, NZ), sds(3, 2, NY, NZ)],
        in_specs=[scalars(), scalars(), whole(), whole(), hbm()] + [anywhere()] * len(before),
        out_specs=[whole()] * 3,
        scratch_shapes=[pltpu.SemaphoreType.DMA((2,))],
        compiler_params=params(),
    )(info, table, atlas, labels, velocity, *before)


def image_edges(info, tile, ra, rb):
    def kernel(info, tile, ra, rb, win, ec, ed):
        px, py = info[2], info[3]
        win[0:CX] = tile[...]
        win[pl.ds(jnp.where(px == 0, CX, WX - DEPTH), DEPTH)] = ra[...]
        win[pl.ds(jnp.where(px == 0, WX - DEPTH, CX), DEPTH)] = rb[...]
        sub = rows8()

        def one(i, carry):
            def tile_of(key):
                return win[i + key, 0:8], win[i + key, 8:16]

            top, bottom = pack_edges(((0, 4, 0), (12, 4, 4)), tile_of, sub)
            ec[i] = jnp.where(py == 0, top, bottom)
            ed[i] = jnp.where(py == 0, bottom, top)
            return carry

        lax.fori_loop(0, 12, one, 0)

    return pl.pallas_call(
        kernel,
        out_shape=[sds(WX, CY, NZ), sds(12, 8, NZ), sds(12, 8, NZ)],
        in_specs=[scalars()] + [whole()] * 3,
        out_specs=[whole()] * 3,
        compiler_params=params(),
    )(info, tile, ra, rb)


def faces(info, own, got, tile, *before):
    def kernel(info, own, *refs):
        got, tile = refs[:9], refs[9]
        vt, ea, eb, la, lb, count, isem, sem = refs[10 + len(before) :]
        count[...] = jnp.full((8, NZ), info[4], jnp.int32).astype(F32)
        px = info[2]
        started = [pltpu.make_async_copy(own, vt.at[info[1]], isem.at[9])]
        for n, (block, t) in enumerate(zip(got, origins(info))):
            if n < 5:
                target = vt.at[t]
            else:
                target = vt.at[t, 0:HALF] if n < 7 else vt.at[t, HALF:VBLOCKS]
            started.append(pltpu.make_async_copy(block, target, isem.at[n]))
        for copy in started:
            copy.start()
        ea[FACE : FACE + DEPTH] = tile[pl.ds(jnp.where(px == 0, CX - DEPTH, 0), DEPTH)]
        eb[FACE : FACE + DEPTH] = tile[pl.ds(jnp.where(px == 0, 0, CX - DEPTH), DEPTH)]
        wait_all(started)
        for g, (to_a, to_b) in enumerate(((ea, eb), (la, lb))):
            for d in range(3):
                for j, k, off in V_SLOTS:
                    top = jnp.where(px == 0, CX - k, 0) + d * CX
                    bottom = jnp.where(px == 0, 0, CX - k) + d * CX
                    row = d * V_ROWS + off
                    to_a[row : row + k] = vt[4 * g + j, pl.ds(top, k)]
                    to_b[row : row + k] = vt[4 * g + j, pl.ds(bottom, k)]

    return pl.pallas_call(
        kernel,
        out_shape=[sds(NT, VBLOCKS, CY, NZ)] + [sds(FACE + DEPTH, CY, NZ)] * 2 + [sds(FACE, CY, NZ)] * 2 + [sds(8, NZ)],
        in_specs=[scalars()] + [anywhere()] * 10 + [whole()] + [anywhere()] * len(before),
        out_specs=[whole()] * 6,
        scratch_shapes=[pltpu.SemaphoreType.DMA((10,)), pltpu.SemaphoreType.DMA((36,))],
        compiler_params=params(),
    )(info, own, *got, tile, *before)


def velocity_edges(info, vt, ra, rb, group, tile=None):
    with_image = tile is not None
    rows = VX + 4 if with_image else VX

    def kernel(info, vt, ra, rb, *refs):
        ec, ed = refs[-2:]
        px, py = info[2], info[3]
        sub = rows8()

        def emit(d, i, slots, tile_of):
            top, bottom = pack_edges(slots, tile_of, sub)
            ec[d, i] = jnp.where(py == 0, top, bottom)
            ed[d, i] = jnp.where(py == 0, bottom, top)

        def halves(value):
            return value[0:8], value[8:16]

        def one(i, carry):
            d, x = lax.div(i, CX // 2), 2 * lax.rem(i, CX // 2)
            for r in range(2):
                row = d * CX + x + r
                emit(d, x + r, V_SLOTS, lambda j: (vt[4 * group + j, row, 0:8], vt[4 * group + j, row, 8:16]))
            return carry

        lax.fori_loop(0, 3 * CX // 2, one, 0)
        for d in range(3):
            base = d * V_ROWS
            for i in range(3):
                up, down = [], []
                for j, k, off in V_SLOTS:
                    if i < k:
                        up.append((j, k, off))
                    if i >= 3 - k:
                        down.append((j, k, off))

                def tile_up(j):
                    row = base + V_SLOTS[j][2] + i
                    return halves(jnp.where(px == 0, ra[row], rb[row]))

                def tile_down(j):
                    row = base + V_SLOTS[j][2] + i - (3 - V_SLOTS[j][1])
                    return halves(jnp.where(px == 0, rb[row], ra[row]))

                emit(d, CX + i, up, tile_up)
                emit(d, CX + 3 + i, down, tile_down)
            if with_image:
                own = refs[0]
                for i in range(4):
                    a, b = ra[FACE + i], rb[FACE + i]
                    other = own[12 + i] if d == 0 else jnp.where(px == d - 1, a, b)
                    pair = (halves(own[4 * d + i]), halves(other))
                    emit(d, VX + i, ((0, 4, 0), (1, 4, 4)), lambda key: pair[key])

    return pl.pallas_call(
        kernel,
        out_shape=[sds(3, rows, 8, NZ)] * 2,
        in_specs=[scalars()] + [whole()] * (4 if with_image else 3),
        out_specs=[whole()] * 2,
        compiler_params=params(),
    )(info, vt, ra, rb, *((tile,) if with_image else ()))


def forward_first(info, tile, vt, ra, rb, yc, yd):
    def kernel(info, tile, vt, ra, rb, yc, yd, pack, ea, eb, i4, vw, image, halos, hsem, sem, osem):
        px, py = info[2], info[3]
        pair = copies([(ra.at[FACE : FACE + DEPTH], halos.at[0]), (rb.at[FACE : FACE + DEPTH], halos.at[1])], hsem)
        started = fill_velocity(0, info, vt, ra, rb, yc, yd, vw, sem)
        image[0, 0:CX, 0:CY] = tile[...]
        wait_all(pair)
        image[0, pl.ds(jnp.where(px == 0, CX, WX - DEPTH), DEPTH), 0:CY] = halos[0]
        image[0, pl.ds(jnp.where(px == 0, WX - DEPTH, CX), DEPTH), 0:CY] = halos[1]
        sub = rows8()
        for j in range(12):
            c, e = yc[j // 4, VX + j % 4], yd[j // 4, VX + j % 4]
            above = jnp.where(py == 0, c, e)
            below = jnp.where(py == 0, e, c)
            image[0, j, CY:WY] = halo_block(above, below, 4, 0, sub)
            image[0, j + 12, CY:WY] = halo_block(above, below, 4, 4, sub)
        wait_all(started)
        out = []
        for j in range(4):
            advance(image.at[j], image.at[j + 1], vw, j, 3 - j)
            out.append(pltpu.make_async_copy(image.at[j, 0:CX, 0:CY], pack.at[j, 0:CX], osem.at[j]))
            out[-1].start()
        last = image.at[4]
        i4[...] = last[0:CX, 0:CY]
        ea[...] = last[pl.ds(jnp.where(px == 0, CX - DEPTH, 0), DEPTH), 0:CY]
        eb[...] = last[pl.ds(jnp.where(px == 0, 0, CX - DEPTH), DEPTH), 0:CY]
        wait_all(out)

    return pl.pallas_call(
        kernel,
        out_shape=[
            sds(NT, PBLOCKS, CY, NZ),
            sds(DEPTH, CY, NZ),
            sds(DEPTH, CY, NZ),
            sds(CX, CY, NZ),
            sds(4, 3, WX, WY, NZ),
        ],
        in_specs=[scalars()] + [whole()] * 6,
        out_specs=[hbm()] + [whole()] * 4,
        scratch_shapes=[
            VMEM((5, WX, WY, NZ), F32),
            VMEM((2, DEPTH, CY, NZ), F32),
            pltpu.SemaphoreType.DMA((2,)),
            pltpu.SemaphoreType.DMA((FILL_COPIES,)),
            pltpu.SemaphoreType.DMA((4,)),
        ],
        compiler_params=params(),
    )(info, tile, vt, ra, rb, yc, yd)


def window(info, vt, ra, rb, yc, yd, group):
    def kernel(info, vt, ra, rb, yc, yd, vw, sem):
        wait_all(fill_velocity(group, info, vt, ra, rb, yc, yd, vw, sem))

    return pl.pallas_call(
        kernel,
        out_shape=sds(4, 3, WX, WY, NZ),
        in_specs=[scalars()] + [whole()] * 5,
        out_specs=whole(),
        scratch_shapes=[pltpu.SemaphoreType.DMA((FILL_COPIES,))],
        compiler_params=params(),
    )(info, vt, ra, rb, yc, yd)


def send_rows(info, widths, source, ea, eb):
    px = info[2]
    off = 0
    for n, k in enumerate(widths):
        top = jnp.where(px == 0, CX, WX - k)
        bottom = jnp.where(px == 0, WX - k, CX)
        ea[off : off + k] = source(n)[pl.ds(top, k)]
        eb[off : off + k] = source(n)[pl.ds(bottom, k)]
        off += k


MID_WIDTHS = (4, 3, 2, 1)
MID_SLOTS = ((0, 4, 0), (1, 3, 4), (3, 1, 7))
END_WIDTHS = (3, 2, 1)
END_SLOTS = ((0, 3, 0), (1, 2, 3), (2, 1, 5), (3, 2, 6))


def forward_second(info, win, ic, idd, target, vw, pack, *before):
    def kernel(info, win, ic, idd, target, vw, pack_in, *refs):
        pack, lw, ea, eb, image, lam, osem = refs[len(before) :]
        fill_image(info, win, ic, idd, image.at[0])
        for n in range(4):
            clear_halo(lam.at[n])
        out = []
        for j in range(4):
            advance(image.at[j], image.at[j + 1], vw, j, 3 - j)
            out.append(pltpu.make_async_copy(image.at[j, 0:CX, 0:CY], pack.at[4 + j, 0:CX], osem.at[j]))
            out[-1].start()
        count = info[4]
        inside = lax.broadcasted_iota(jnp.int32, (CY, NZ), 0) * NZ + lax.broadcasted_iota(jnp.int32, (CY, NZ), 1)
        zero = jnp.zeros((8, NZ), F32)

        def one(x, carry):
            value = image[4, x, 0:CY] - target[x]
            lam[0, x, 0:CY] = jnp.where(inside + x * (CY * NZ) < count, value, 0.0)
            lam[0, x, CY:WY] = zero
            return carry

        lax.fori_loop(0, CX, one, 0)
        out.append(pltpu.make_async_copy(lam.at[0, 0:CX, 0:CY], pack.at[7, CX : 2 * CX], osem.at[4]))
        out[-1].start()
        for n in range(4):
            scatter(lam.at[n], lam.at[n + 1], vw, 3 - n, n + 1)
        for n in range(4):
            lw[n] = lam[4 - n, 0:CX]
        send_rows(info, MID_WIDTHS, lambda n: lam.at[4 - n], ea, eb)
        wait_all(out)

    return pl.pallas_call(
        kernel,
        out_shape=[sds(NT, PBLOCKS, CY, NZ), sds(4, CX, WY, NZ), sds(10, WY, NZ), sds(10, WY, NZ)],
        in_specs=[scalars()] + [whole()] * 5 + [hbm()] + [anywhere()] * len(before),
        out_specs=[hbm()] + [whole()] * 3,
        scratch_shapes=[
            VMEM((5, WX, WY, NZ), F32),
            VMEM((5, WX, WY, NZ), F32),
            pltpu.SemaphoreType.DMA((5,)),
        ],
        input_output_aliases={6: 0},
        compiler_params=params(),
    )(info, win, ic, idd, target, vw, pack, *before)


def costate_edges(info, lw, ra, rb, widths, slots, *before):
    def kernel(info, lw_in, ra, rb, *refs):
        lw, ec, ed = refs[len(before) :]
        px, py = info[2], info[3]
        off = 0
        for n, k in enumerate(widths):
            for i in range(k):
                to_a = jnp.where(px == 0, CX - k, 0) + i
                to_b = jnp.where(px == 0, 0, CX - k) + i
                lw[n, to_a] = lw[n, to_a] + ra[off + i]
                lw[n, to_b] = lw[n, to_b] + rb[off + i]
            off += k
        sub = rows8()

        def one(x, carry):
            top = jnp.zeros((8, NZ), F32)
            bottom = top
            for n, k, off in slots:
                block = lw[n, x, CY:WY]
                top = put(top, block, off, off, off + k, sub)
                bottom = put(bottom, block, off + k, off, off + k, sub)
            ec[x] = jnp.where(py == 0, top, bottom)
            ed[x] = jnp.where(py == 0, bottom, top)
            return carry

        lax.fori_loop(0, CX, one, 0)

    return pl.pallas_call(
        kernel,
        out_shape=[sds(4, CX, WY, NZ), sds(CX, 8, NZ), sds(CX, 8, NZ)],
        in_specs=[scalars()] + [whole()] * 3 + [anywhere()] * len(before),
        out_specs=[whole()] * 3,
        input_output_aliases={1: 0},
        compiler_params=params(),
    )(info, lw, ra, rb, *before)


def take(c, e, py, k, off, sub):
    below = jnp.where(py == 0, e, c)
    above = jnp.where(py == 0, c, e)
    zero = jnp.zeros((8, NZ), F32)
    return put(zero, below, -off, 0, k, sub), put(zero, above, 8 - k - off, 8 - k, 8, sub)


def backward_second(info, lw, lc, ld, vw, pack, *before):
    def kernel(info, lw, lc, ld, vw, pack_in, *refs):
        pack, lw2, ea, eb, lam, done, osem = refs[len(before) :]
        for n in range(3):
            clear_halo(lam.at[n])
        py = info[3]
        sub = rows8()
        zero = jnp.zeros((8, NZ), F32)

        def one(x, carry):
            c, e = lc[x], ld[x]
            for n, k, off in MID_SLOTS:
                low, high = take(c, e, py, k, off, sub)
                low, high = lw[n, x, 0:8] + low, lw[n, x, 8:16] + high
                if n == 0:
                    lam[0, x, 0:8] = low
                    lam[0, x, 8:16] = high
                    lam[0, x, CY:WY] = zero
                else:
                    done[(n - 1) // 2, x, 0:8] = low
                    done[(n - 1) // 2, x, 8:16] = high
            return carry

        lax.fori_loop(0, CX, one, 0)
        out = [
            pltpu.make_async_copy(lam.at[0, 0:CX, 0:CY], pack.at[3, CX : 2 * CX], osem.at[0]),
            pltpu.make_async_copy(done.at[0], pack.at[4, CX : 2 * CX], osem.at[1]),
            pltpu.make_async_copy(done.at[1], pack.at[6, CX : 2 * CX], osem.at[2]),
        ]
        for copy in out:
            copy.start()
        for n in range(3):
            scatter(lam.at[n], lam.at[n + 1], vw, 3 - n, n + 1)
        for n in range(3):
            lw2[n] = lam[3 - n, 0:CX]
        lw2[3] = lw[2]
        send_rows(info, END_WIDTHS, lambda n: lam.at[3 - n], ea, eb)
        wait_all(out)

    return pl.pallas_call(
        kernel,
        out_shape=[sds(NT, PBLOCKS, CY, NZ), sds(4, CX, WY, NZ), sds(6, WY, NZ), sds(6, WY, NZ)],
        in_specs=[scalars()] + [whole()] * 4 + [hbm()] + [anywhere()] * len(before),
        out_specs=[hbm()] + [whole()] * 3,
        scratch_shapes=[
            VMEM((4, WX, WY, NZ), F32),
            VMEM((2, CX, CY, NZ), F32),
            pltpu.SemaphoreType.DMA((3,)),
        ],
        input_output_aliases={5: 0},
        compiler_params=params(),
    )(info, lw, lc, ld, vw, pack, *before)


def costate_finish(info, lw, lc, ld, total, pack):
    def kernel(info, lw, lc, ld, total, pack_in, pack, done, note, sem):
        note[0] = jnp.broadcast_to(total[0:1], (CY, NZ))
        started = copies([(note, pack.at[t, 2 * CX : PBLOCKS]) for t in range(NT)], sem.at[pl.ds(4, NT)])
        py = info[3]
        sub = rows8()

        def one(x, carry):
            c, e = lc[x], ld[x]
            for n, k, off in END_SLOTS:
                low, high = take(c, e, py, k, off, sub)
                done[n, x, 0:8] = lw[n, x, 0:8] + low
                done[n, x, 8:16] = lw[n, x, 8:16] + high
            return carry

        lax.fori_loop(0, CX, one, 0)
        wait_all(copies([(done.at[n], pack.at[m, CX : 2 * CX]) for n, m in enumerate((0, 1, 2, 5))], sem))
        wait_all(started)

    return pl.pallas_call(
        kernel,
        out_shape=sds(NT, PBLOCKS, CY, NZ),
        in_specs=[scalars()] + [whole()] * 4 + [hbm()],
        out_specs=hbm(),
        scratch_shapes=[VMEM((4, CX, CY, NZ), F32), VMEM((1, CY, NZ), F32), pltpu.SemaphoreType.DMA((4 + NT,))],
        input_output_aliases={5: 0},
        compiler_params=params(58),
    )(info, lw, lc, ld, total, pack)


PAD = 8
PY = NY + 2 * PAD
CHUNK = 32


def clear_pads(ref, lead):
    zero = jnp.zeros((PAD, NZ), F32)
    for index in lead:
        ref[(*index, slice(0, PAD))] = zero
        ref[(*index, slice(PAD + NY, PY))] = zero


def part(ref, index, y, move=0):
    return ref[(*index, slice(PAD + y + move, PAD + y + move + CHUNK))]


def smooth(ref, before, at, after, y, m):
    first, last = m
    c = part(ref, at, y)
    near = part(ref, before, y) + part(ref, after, y)
    near += part(ref, at, y, -1) + part(ref, at, y, 1)
    near += jnp.where(first, 0.0, pltpu.roll(c, 1, 1)) + jnp.where(last, 0.0, pltpu.roll(c, NZ - 1, 1))
    return (1.0 - 6.0 * KAPPA) * c + KAPPA * near


def slope(v, ref, before, at, after, direction, y, m):
    first, last = m
    c = part(ref, at, y)
    if direction == 0:
        behind, beyond = part(ref, before, y), part(ref, after, y)
    elif direction == 1:
        behind, beyond = part(ref, at, y, -1), part(ref, at, y, 1)
    else:
        behind = jnp.where(first, 0.0, pltpu.roll(c, 1, 1))
        beyond = jnp.where(last, 0.0, pltpu.roll(c, NZ - 1, 1))
    return jnp.where(v > 0.0, c - behind, beyond - c)


CHUNKS = tuple(range(0, NY, CHUNK))


def coefficient(notes, cells):
    total = notes[0, 0, 0:8]
    for c in range(1, NY // CY):
        total += notes[c, 0, 0:8]
    return ((-STEP * DATA_WEIGHT) * (cells / total))[0:1]


def finish_inside(velocity, pack, cells):
    def kernel(vel, pack, out, keep_c, keep_s, islab, lslab, grad, soft, notes, sem):
        d = pl.program_id(0)

        @pl.when(d == 0)
        def _():
            pairs = []
            for c in range(NY // CY):
                y = slice(c * CY, (c + 1) * CY)
                padded = slice(PAD + c * CY, PAD + (c + 1) * CY)
                pairs += [
                    (pack.at[c, 0:CX], islab.at[:, padded]),
                    (pack.at[c, CX : 2 * CX], lslab.at[:, y]),
                    (pack.at[c, 2 * CX : PBLOCKS], notes.at[c]),
                ]
            started = copies(pairs, sem)
            for ref in (islab, grad, soft):
                clear_pads(ref, [(x,) for x in range(CX)])
            wait_all(started)

        coef = coefficient(notes, cells)
        m = lane_masks((CHUNK, NZ))
        for direction in range(3):

            @pl.when(d == direction)
            def _(direction=direction):
                def one(x, carry):
                    for y in CHUNKS:
                        rows = slice(y, y + CHUNK)
                        g = slope(vel[0, 0, x, rows], islab, (x - 1,), (x,), (x + 1,), direction, y, m)
                        grad[x, PAD + y : PAD + y + CHUNK] = (coef * lslab[x, rows]) * g
                    return carry

                lax.fori_loop(1, CX - 1, one, 0)

        def once(x, carry):
            for y in CHUNKS:
                soft[x, PAD + y : PAD + y + CHUNK] = smooth(grad, (x - 1,), (x,), (x + 1,), y, m)
            return carry

        lax.fori_loop(2, CX - 2, once, 0)

        def twice(x, carry):
            for y in CHUNKS:
                rows = slice(y, y + CHUNK)
                out[0, 0, x, rows] = vel[0, 0, x, rows] + smooth(soft, (x - 1,), (x,), (x + 1,), y, m)
            return carry

        lax.fori_loop(3, CX - 3, twice, 0)
        for n, (x, y) in enumerate(((1, 2), (2, 3), (13, 12), (14, 13))):
            keep_c[0, n] = grad[x, PAD : PAD + NY]
            keep_s[0, n] = soft[y, PAD : PAD + NY]

    slab = pl.BlockSpec((1, 1, CX, NY, NZ), lambda d: (0, d, 0, 0, 0))
    kept = pl.BlockSpec((1, 4, NY, NZ), lambda d: (d, 0, 0, 0))
    return pl.pallas_call(
        kernel,
        grid=(3,),
        out_shape=[sds(1, 3, CX, NY, NZ), sds(3, 4, NY, NZ), sds(3, 4, NY, NZ)],
        in_specs=[slab, hbm()],
        out_specs=[slab, kept, kept],
        scratch_shapes=[VMEM((CX, PY, NZ), F32), VMEM((CX, NY, NZ), F32), VMEM((CX, PY, NZ), F32), VMEM((CX, PY, NZ), F32)]
        + [VMEM((8, 1, CY, NZ), F32), pltpu.SemaphoreType.DMA((24,))],
        compiler_params=params(60),
    )(velocity, pack)


def finish_edges(info, velocity, va, vb, pack, fa, fb, keep_c, keep_s, partial, cells):
    def kernel(info, vel, va, vb, pack, fa, fb, keep_c, keep_s, partial, out, slabs, all_rows, grad, soft, all_results, notes, sem, osem):
        d = pl.program_id(0)
        px = info[2]

        @pl.when(d == 0)
        def _():
            pairs = []
            above, below = jnp.where(px == 0, 1, 0), jnp.where(px == 0, 0, 1)
            hi, hl = jnp.where(px == 0, 2, 0), jnp.where(px == 0, 6, 5)
            bi, bl = jnp.where(px == 0, 0, 2), jnp.where(px == 0, 5, 6)
            for c in range(NY // CY):
                y = slice(PAD + c * CY, PAD + (c + 1) * CY)
                pairs += [
                    (pack.at[c, 0:2], slabs.at[0, 3:5, y]),
                    (pack.at[c, CX : CX + 1], slabs.at[0, 7:8, y]),
                    (pack.at[c, CX - 2 : CX], slabs.at[1, 0:2, y]),
                    (pack.at[c, 2 * CX - 1 : 2 * CX], slabs.at[1, 5:6, y]),
                    (pack.at[c, 2 * CX : PBLOCKS], notes.at[c]),
                    (fa.at[c, 0:3], slabs.at[above, pl.ds(hi, 3), y]),
                    (fa.at[c, 3:5], slabs.at[above, pl.ds(hl, 2), y]),
                    (fb.at[c, 0:3], slabs.at[below, pl.ds(bi, 3), y]),
                    (fb.at[c, 3:5], slabs.at[below, pl.ds(bl, 2), y]),
                ]
            for n in range(3):
                pairs += [(vel.at[0, n, 0:3], all_rows.at[n, 0]), (vel.at[0, n, CX - 3 : CX], all_rows.at[n, 1])]
            started = copies(pairs, sem)
            clear_pads(slabs, [(side, n) for side in range(2) for n in range(5)])
            for ref in (grad, soft):
                clear_pads(ref, [(side, n) for side in range(2) for n in range(5)])
            wait_all(started)

        vrows, result = all_rows.at[d], all_results.at[d]

        coef = coefficient(notes, cells)
        m = lane_masks((CHUNK, NZ))
        for direction in range(3):

            @pl.when(d == direction)
            def _(direction=direction):
                for side in range(2):
                    for n in range(3):
                        own = n == 2 if side == 0 else n == 0
                        for y in CHUNKS:
                            rows = slice(y, y + CHUNK)
                            if own:
                                v = vrows[0, 0, rows] if side == 0 else vrows[1, 2, rows]
                            else:
                                k = n if side == 0 else n - 1
                                v = jnp.where((px == 0) == (side == 1), va[0, k, rows], vb[0, k, rows])
                            g = slope(v, slabs, (side, n), (side, n + 1), (side, n + 2), direction, y, m)
                            grad[side, n, PAD + y : PAD + y + CHUNK] = (coef * part(slabs, (side, 5 + n), y)) * g

        inner = slice(PAD, PAD + NY)
        for n in range(2):
            grad[0, 3 + n, inner] = keep_c[0, n]
            grad[1, 3 + n, inner] = keep_c[0, 2 + n]
            soft[0, 3 + n, inner] = keep_s[0, n]
            soft[1, n, inner] = keep_s[0, 2 + n]
        zero = jnp.zeros((NY, NZ), F32)
        for side in range(2):
            order = [0, 1, 2, 3, 4] if side == 0 else [3, 4, 0, 1, 2]
            for n in range(3):
                at = [(side, order[n + k]) for k in range(3)]
                for y in CHUNKS:
                    soft[side, n + 2 * side, PAD + y : PAD + y + CHUNK] = smooth(grad, *at, y, m)

        @pl.when(info[0] == 0)
        def _():
            soft[0, 0, inner] = zero

        @pl.when(info[0] == info[5] - 1)
        def _():
            soft[1, 4, inner] = zero

        for side in range(2):
            for n in range(3):
                for y in CHUNKS:
                    rows = slice(y, y + CHUNK)
                    value = smooth(soft, (side, n), (side, n + 1), (side, n + 2), y, m)
                    result[side, n, rows] = vrows[side, n, rows] + value

        def leave(n):
            low, high = all_results.at[n, 0], all_results.at[n, 1]
            return [
                pltpu.make_async_copy(low, out.at[0, n, 0:3], osem.at[n, 0]),
                pltpu.make_async_copy(high, out.at[0, n, CX - 3 : CX], osem.at[n, 1]),
            ]

        for n in range(3):

            @pl.when(d == n)
            def _(n=n):
                for copy in leave(n):
                    copy.start()

        @pl.when(d == 2)
        def _():
            for n in range(3):
                wait_all(leave(n))

    face = pl.BlockSpec((1, 2, NY, NZ), lambda d: (d, 0, 0, 0))
    kept = pl.BlockSpec((1, 4, NY, NZ), lambda d: (d, 0, 0, 0))
    return pl.pallas_call(
        kernel,
        grid=(3,),
        out_shape=sds(1, 3, CX, NY, NZ),
        in_specs=[scalars(), hbm(), face, face] + [hbm()] + [anywhere()] * 2 + [kept, kept, hbm()],
        out_specs=hbm(),
        scratch_shapes=[
            VMEM((2, 8, PY, NZ), F32),
            VMEM((3, 2, 3, NY, NZ), F32),
            VMEM((2, 5, PY, NZ), F32),
            VMEM((2, 5, PY, NZ), F32),
            VMEM((3, 2, 3, NY, NZ), F32),
            VMEM((8, 1, CY, NZ), F32),
            pltpu.SemaphoreType.DMA((78,)),
            pltpu.SemaphoreType.DMA((3, 2)),
        ],
        input_output_aliases={9: 0},
        compiler_params=params(60),
    )(info, velocity, va, vb, pack, fa, fb, keep_c, keep_s, partial)


def edge_rows(value, dim, k, px):
    length = value.shape[dim]
    high = lax.slice_in_dim(value, length - k, length, axis=dim)
    low = lax.slice_in_dim(value, 0, k, axis=dim)
    return jnp.where(px == 0, high, low), jnp.where(px == 0, low, high)


def shards(velocity, atlas_image, target, labels, label_table, counts):
    s, c = lax.axis_index("space"), lax.axis_index("cuts")
    px, py = s % 2, c % 2
    info = jnp.stack([s, c, px, py, counts[0], jnp.int32(lax.axis_size("space")), s, s]).astype(jnp.int32)
    far_a, far_b, *direct = repack(info, velocity)
    got, far = spread(far_a, far_b, direct[:5])

    tile, ova, ovb = template(info, label_table, atlas_image, labels, velocity, far)
    ova, ovb = swap(ova, ovb, "space")

    vt, fa, fb, ga, gb, total = faces(info, direct[5], got, tile, ova, ovb)
    fa, fb = swap(fa, fb, "space")
    ga, gb = swap(ga, gb, "space")
    y0 = swap(*velocity_edges(info, vt, fa, fb, 0, tile), "cuts")
    total = xor_swap(total, 1)
    y1 = swap(*velocity_edges(info, vt, ga, gb, 1), "cuts")
    pack, ea, eb, i4, vw0 = forward_first(info, tile, vt, fa, fb, *y0)
    win, ec, ed = image_edges(info, i4, *swap(ea, eb, "space"))
    vw1 = window(info, vt, ga, gb, *y1, 1)
    ic, idd = swap(ec, ed, "cuts")
    pack, lw, ea, eb = forward_second(info, win, ic, idd, target, vw1, pack, total)
    total = xor_swap(total, 2)
    lw, ec, ed = costate_edges(info, lw, *swap(ea, eb, "space"), MID_WIDTHS, MID_SLOTS, total)
    total = xor_swap(total, 4)
    ec, ed = swap(ec, ed, "cuts")
    pack, lw, ea, eb = backward_second(info, lw, ec, ed, vw0, pack, total)
    total = xor_swap(total, 8)
    lw, ec, ed = costate_edges(info, lw, *swap(ea, eb, "space"), END_WIDTHS, END_SLOTS)
    ec, ed = swap(ec, ed, "cuts")
    pack = costate_finish(info, lw, ec, ed, total, pack)
    pack = lax.all_to_all(pack, "cuts", split_axis=0, concat_axis=0, tiled=True)

    cells = float(CX * CY * NZ * lax.axis_size("space") * lax.axis_size("cuts"))
    rows = [jnp.concatenate([pack[:, a : a + 3], pack[:, b : b + 2]], axis=1) for a, b in ((CX - 3, 2 * CX - 2), (0, CX))]
    ea, eb = jnp.where(px == 0, rows[0], rows[1]), jnp.where(px == 0, rows[1], rows[0])
    fa, fb = swap(ea, eb, "space")
    partial, keep_c, keep_s = finish_inside(velocity, pack, cells)
    return finish_edges(info, velocity, ova, ovb, pack, fa, fb, keep_c, keep_s, partial, cells)


def solution(mesh):
    in_specs = (
        P("cuts", None, "space", None, None),
        P("space", "cuts", None),
        P("space", "cuts", None),
        P("space", "cuts", None),
        P(),
        P(("space", "cuts")),
    )
    out_specs = P("cuts", None, "space", None, None)
    return jax.shard_map(shards, mesh=mesh, in_specs=in_specs, out_specs=out_specs, check_vma=False)
```

```python
import functools

import jax
import jax.numpy as jnp
from jax import lax
from jax.experimental import pallas as pl
from jax.experimental.pallas import tpu as pltpu
from jax.sharding import PartitionSpec as P

F32 = jnp.float32
NT = 8
STEP = 1.0 / NT
DATA_WEIGHT = 4.0
KAPPA = 0.125
CX, CY, NZ = 16, 16, 256
NY = 128
DEPTH = 4
WX, WY = CX + 2 * DEPTH, CY + 2 * DEPTH
V_SLOTS = ((0, 3, 0), (1, 2, 3), (2, 1, 5))
V_ROWS = 6
VX = CX + 6
VBLOCKS = 3 * CX
PBLOCKS = 2 * CX + 1
HALF = VBLOCKS // 2
RING = 4
FACE = 3 * V_ROWS
VMEM = pltpu.VMEM
ANY = pl.ANY


def whole():
    return pl.BlockSpec(memory_space=VMEM)


def anywhere():
    return pl.BlockSpec(memory_space=ANY)


def hbm():
    return pl.BlockSpec(memory_space=pltpu.HBM)


def scalars():
    return pl.BlockSpec(memory_space=pltpu.SMEM)


def params(mib=16):
    return pltpu.CompilerParams(vmem_limit_bytes=mib * 1024 * 1024)


def sds(*shape):
    return jax.ShapeDtypeStruct(shape, F32)


def swaps(size, first):
    pairs = []
    for i in range(first, size - 1, 2):
        pairs += [(i, i + 1), (i + 1, i)]
    return pairs


def swap(even, odd, axis):
    size = lax.axis_size(axis)
    return lax.ppermute(even, axis, swaps(size, 0)), lax.ppermute(odd, axis, swaps(size, 1))


def xor_swap(value, reach):
    size = lax.axis_size("space")
    return value + lax.ppermute(value, "space", [(i, i ^ reach) for i in range(size)])


def rows8():
    return lax.broadcasted_iota(jnp.int32, (8, NZ), 0)


def turn(block, shift):
    shift = shift % 8
    return pltpu.roll(block, shift, 0) if shift else block


def put(total, block, shift, low, high, sub):
    return jnp.where((sub >= low) & (sub < high), turn(block, shift), total)


def pack_edges(slots, tile, sub):
    top = jnp.zeros((8, NZ), F32)
    bottom = top
    for key, k, off in slots:
        low8, high8 = tile(key)
        top = put(top, high8, off + k, off, off + k, sub)
        bottom = put(bottom, low8, off, off, off + k, sub)
    return top, bottom


def halo_block(above, below, k, off, sub):
    block = put(jnp.zeros((8, NZ), F32), above, -off, 0, k, sub)
    return put(block, below, 8 - k - off, 8 - k, 8, sub)


def lane_masks(shape):
    z = lax.broadcasted_iota(jnp.int32, shape, 1)
    return z == 0, z == NZ - 1


def copies(pairs, sem):
    started = [pltpu.make_async_copy(a, b, sem.at[i]) for i, (a, b) in enumerate(pairs)]
    for copy in started:
        copy.start()
    return started


def wait_all(started):
    for copy in started:
        copy.wait()


def fill_velocity(group, info, vt, ra, rb, yc, yd, vw, sem):
    px, py = info[2], info[3]
    pairs = []
    for d in range(3):
        for j in range(4):
            pairs.append((vt.at[4 * group + j, d * CX : (d + 1) * CX], vw.at[j, d, 0:CX, 0:CY]))
        for j, k, off in V_SLOTS:
            to_a = jnp.where(px == 0, CX, WX - k)
            to_b = jnp.where(px == 0, WX - k, CX)
            row = d * V_ROWS + off
            pairs.append((ra.at[row : row + k], vw.at[j, d, pl.ds(to_a, k), 0:CY]))
            pairs.append((rb.at[row : row + k], vw.at[j, d, pl.ds(to_b, k), 0:CY]))
    started = copies(pairs, sem)
    sub = rows8()
    zero_row = jnp.zeros((WY, NZ), F32)
    zero_tile = jnp.zeros((8, NZ), F32)
    for j in range(4):
        k = 3 - j
        for d in range(3):
            for x in range(CX + k, WX - k):
                vw[j, d, x] = zero_row

    def blocks(d, i, x, keep):
        c, e = yc[d, i], yd[d, i]
        above = jnp.where(py == 0, c, e)
        below = jnp.where(py == 0, e, c)
        for j, k, off in V_SLOTS:
            if keep(k):
                vw[j, d, x, CY:WY] = halo_block(above, below, k, off, sub)

    def one(i, carry):
        for d in range(3):
            for r in range(2):
                blocks(d, 2 * i + r, 2 * i + r, lambda k: True)
                vw[3, d, 2 * i + r, CY:WY] = zero_tile
        return carry

    lax.fori_loop(0, CX // 2, one, 0)
    for i in range(CX, VX):
        x = i if i < CX + 3 else i + 2
        for d in range(3):
            blocks(d, i, x, lambda k: x < CX + k or x >= WX - k)
    return started


FILL_COPIES = 30


def fill_image(info, win, yc, yd, image):
    py = info[3]
    sub = rows8()

    def one(i, carry):
        c, e = yc[i], yd[i]
        above = jnp.where(py == 0, c, e)
        below = jnp.where(py == 0, e, c)
        image[i, 0:CY] = win[i]
        image[i + 12, 0:CY] = win[i + 12]
        image[i, CY:WY] = halo_block(above, below, 4, 0, sub)
        image[i + 12, CY:WY] = halo_block(above, below, 4, 4, sub)
        return carry

    lax.fori_loop(0, 12, one, 0)


ROWS = 2


def sweep_rows(reach, row, dst):
    turns = -(-(CX + 2 * reach) // ROWS)

    def one(i, carry):
        xs = [lax.rem(i * ROWS + r - reach + WX, WX) for r in range(ROWS)]
        values = [row(x, lax.rem(x + WX - 1, WX), lax.rem(x + 1, WX)) for x in xs]
        for x, value in zip(xs, values):
            dst[x] = value
        return carry

    lax.fori_loop(0, turns, one, 0)


def advance(src, dst, vw, j, reach):
    first, last = lane_masks((WY, NZ))

    def row(x, xm, xp):
        c = src[x]
        v0, v1, v2 = vw[j, 0, x], vw[j, 1, x], vw[j, 2, x]
        flow = v0 * jnp.where(v0 > 0.0, c - src[xm], src[xp] - c)
        flow += v1 * jnp.where(v1 > 0.0, c - pltpu.roll(c, 1, 0), pltpu.roll(c, WY - 1, 0) - c)
        behind = jnp.where(first, 0.0, pltpu.roll(c, 1, 1))
        beyond = jnp.where(last, 0.0, pltpu.roll(c, NZ - 1, 1))
        flow += v2 * jnp.where(v2 > 0.0, c - behind, beyond - c)
        return c - STEP * flow

    sweep_rows(reach, row, dst)


def scatter(src, dst, vw, j, reach):
    first, last = lane_masks((WY, NZ))

    def row(x, xm, xp):
        c = src[x]
        v0, v1, v2 = vw[j, 0, x], vw[j, 1, x], vw[j, 2, x]
        change = (jnp.abs(v0) + jnp.abs(v1) + jnp.abs(v2)) * c
        change -= jnp.maximum(vw[j, 0, xp], 0.0) * src[xp]
        change += jnp.minimum(vw[j, 0, xm], 0.0) * src[xm]
        change -= pltpu.roll(jnp.maximum(v1, 0.0) * c, WY - 1, 0)
        change += pltpu.roll(jnp.minimum(v1, 0.0) * c, 1, 0)
        change -= jnp.where(last, 0.0, pltpu.roll(jnp.maximum(v2, 0.0) * c, NZ - 1, 1))
        change += jnp.where(first, 0.0, pltpu.roll(jnp.minimum(v2, 0.0) * c, 1, 1))
        return c - STEP * change

    sweep_rows(reach, row, dst)


def clear_halo(ref, x_rows=True):
    zero_row = jnp.zeros((WY, NZ), F32)
    for x in range(CX, WX):
        ref[x] = zero_row


def ring_pairs(up, across, size):
    pairs = []
    for i in range(size):
        ring, at = divmod(i, RING)
        pairs.append((i, ((ring + across) % 2) * RING + (at + up) % RING))
    return pairs


def shift(value, up, across):
    return lax.ppermute(value, "cuts", ring_pairs(up, across, lax.axis_size("cuts")))


DIRECT = ((1, 1), (-1, 1), (0, 1), (1, 0), (-1, 0))


def repack(info, velocity):
    def kernel(info, src, far_a, far_b, *refs):
        direct, own = refs[:5], refs[5]
        held, isem, osem = refs[6:]
        ring, at = lax.div(info[1], RING), lax.rem(info[1], RING)

        def start_in(n, up, across):
            c = lax.rem(ring + across, 2) * RING + lax.rem(at + up + RING, RING)
            rows = pl.ds(pl.multiple_of(c * CY, CY), CY)
            for d in range(3):
                copy = pltpu.make_async_copy(src.at[0, d, :, rows], held.at[n, d * CX : (d + 1) * CX], isem.at[n * 3 + d])
                copy.start()
                arrive[n].append(copy)

        order = ((2, 0), (2, 1)) + DIRECT + ((0, 0),)
        arrive = [[] for _ in order]
        for n, (up, across) in enumerate(order):
            start_in(n, up, across)
        leave = []
        for n in range(8):
            wait_all(arrive[n])
            if n < 2:
                pairs = [(held.at[n, 0:HALF], far_a.at[n]), (held.at[n, HALF:VBLOCKS], far_b.at[n])]
            else:
                pairs = [(held.at[n], direct[n - 2] if n < 7 else own)]
            for source, target in pairs:
                copy = pltpu.make_async_copy(source, target, osem.at[len(leave)])
                copy.start()
                leave.append(copy)
        wait_all(leave)

    return pl.pallas_call(
        kernel,
        out_shape=[sds(2, HALF, CY, NZ)] * 2 + [sds(VBLOCKS, CY, NZ)] * 6,
        in_specs=[scalars(), hbm()],
        out_specs=[anywhere()] * 8,
        scratch_shapes=[
            VMEM((8, VBLOCKS, CY, NZ), F32),
            pltpu.SemaphoreType.DMA((24,)),
            pltpu.SemaphoreType.DMA((10,)),
        ],
        compiler_params=params(60),
    )(info, velocity)


def spread(far_a, far_b, direct):
    far_a, far_b = shift(far_a, 1, 0), shift(far_b, -1, 0)
    got = [shift(block, up, across) for block, (up, across) in zip(direct, DIRECT)]
    a = [shift(far_a[n], 1, n) for n in range(2)]
    b = [shift(far_b[n], -1, n) for n in range(2)]
    return got + a + b, far_a


def origins(info):
    ring, at = lax.div(info[1], RING), lax.rem(info[1], RING)
    moves = DIRECT + ((2, 0), (2, 1), (2, 0), (2, 1))
    return [lax.rem(ring + across, 2) * RING + lax.rem(at - up + RING, RING) for up, across in moves]


def template(info, table, atlas, labels, velocity, *before):
    def kernel(info, table, atlas, labels, velocity, *refs):
        tmpl, ea, eb, sem = refs[len(before) :]
        px = info[2]
        top, bottom = jnp.where(px == 0, CX - 2, 0), jnp.where(px == 0, 0, CX - 2)
        started = copies([(velocity.at[0, :, pl.ds(top, 2)], ea), (velocity.at[0, :, pl.ds(bottom, 2)], eb)], sem)

        def one(x, carry):
            lab = labels[x]
            value = jnp.zeros((CY, NZ), F32)
            for l in range(64):
                value = jnp.where(lab == l, table[l], value)
            tmpl[x] = atlas[x] + value
            return carry

        lax.fori_loop(0, CX, one, 0)
        wait_all(started)

    return pl.pallas_call(
        kernel,
        out_shape=[sds(CX, CY, NZ), sds(3, 2, NY, NZ), sds(3, 2, NY, NZ)],
        in_specs=[scalars(), scalars(), whole(), whole(), hbm()] + [anywhere()] * len(before),
        out_specs=[whole()] * 3,
        scratch_shapes=[pltpu.SemaphoreType.DMA((2,))],
        compiler_params=params(),
    )(info, table, atlas, labels, velocity, *before)


def image_edges(info, tile, ra, rb):
    def kernel(info, tile, ra, rb, win, ec, ed):
        px, py = info[2], info[3]
        win[0:CX] = tile[...]
        win[pl.ds(jnp.where(px == 0, CX, WX - DEPTH), DEPTH)] = ra[...]
        win[pl.ds(jnp.where(px == 0, WX - DEPTH, CX), DEPTH)] = rb[...]
        sub = rows8()

        def one(i, carry):
            def tile_of(key):
                return win[i + key, 0:8], win[i + key, 8:16]

            top, bottom = pack_edges(((0, 4, 0), (12, 4, 4)), tile_of, sub)
            ec[i] = jnp.where(py == 0, top, bottom)
            ed[i] = jnp.where(py == 0, bottom, top)
            return carry

        lax.fori_loop(0, 12, one, 0)

    return pl.pallas_call(
        kernel,
        out_shape=[sds(WX, CY, NZ), sds(12, 8, NZ), sds(12, 8, NZ)],
        in_specs=[scalars()] + [whole()] * 3,
        out_specs=[whole()] * 3,
        compiler_params=params(),
    )(info, tile, ra, rb)


def faces(info, own, got, tile, *before):
    def kernel(info, own, *refs):
        got, tile = refs[:9], refs[9]
        vt, ea, eb, la, lb, count, isem, sem = refs[10 + len(before) :]
        count[...] = jnp.full((8, NZ), info[4], jnp.int32).astype(F32)
        px = info[2]
        started = [pltpu.make_async_copy(own, vt.at[info[1]], isem.at[9])]
        for n, (block, t) in enumerate(zip(got, origins(info))):
            if n < 5:
                target = vt.at[t]
            else:
                target = vt.at[t, 0:HALF] if n < 7 else vt.at[t, HALF:VBLOCKS]
            started.append(pltpu.make_async_copy(block, target, isem.at[n]))
        for copy in started:
            copy.start()
        ea[FACE : FACE + DEPTH] = tile[pl.ds(jnp.where(px == 0, CX - DEPTH, 0), DEPTH)]
        eb[FACE : FACE + DEPTH] = tile[pl.ds(jnp.where(px == 0, 0, CX - DEPTH), DEPTH)]
        wait_all(started)
        for g, (to_a, to_b) in enumerate(((ea, eb), (la, lb))):
            for d in range(3):
                for j, k, off in V_SLOTS:
                    top = jnp.where(px == 0, CX - k, 0) + d * CX
                    bottom = jnp.where(px == 0, 0, CX - k) + d * CX
                    row = d * V_ROWS + off
                    to_a[row : row + k] = vt[4 * g + j, pl.ds(top, k)]
                    to_b[row : row + k] = vt[4 * g + j, pl.ds(bottom, k)]

    return pl.pallas_call(
        kernel,
        out_shape=[sds(NT, VBLOCKS, CY, NZ)] + [sds(FACE + DEPTH, CY, NZ)] * 2 + [sds(FACE, CY, NZ)] * 2 + [sds(8, NZ)],
        in_specs=[scalars()] + [anywhere()] * 10 + [whole()] + [anywhere()] * len(before),
        out_specs=[whole()] * 6,
        scratch_shapes=[pltpu.SemaphoreType.DMA((10,)), pltpu.SemaphoreType.DMA((36,))],
        compiler_params=params(),
    )(info, own, *got, tile, *before)


def velocity_edges(info, vt, ra, rb, group, tile=None):
    with_image = tile is not None
    rows = VX + 4 if with_image else VX

    def kernel(info, vt, ra, rb, *refs):
        ec, ed = refs[-2:]
        px, py = info[2], info[3]
        sub = rows8()

        def emit(d, i, slots, tile_of):
            top, bottom = pack_edges(slots, tile_of, sub)
            ec[d, i] = jnp.where(py == 0, top, bottom)
            ed[d, i] = jnp.where(py == 0, bottom, top)

        def halves(value):
            return value[0:8], value[8:16]

        def one(i, carry):
            d, x = lax.div(i, CX // 2), 2 * lax.rem(i, CX // 2)
            for r in range(2):
                row = d * CX + x + r
                emit(d, x + r, V_SLOTS, lambda j: (vt[4 * group + j, row, 0:8], vt[4 * group + j, row, 8:16]))
            return carry

        lax.fori_loop(0, 3 * CX // 2, one, 0)
        for d in range(3):
            base = d * V_ROWS
            for i in range(3):
                up, down = [], []
                for j, k, off in V_SLOTS:
                    if i < k:
                        up.append((j, k, off))
                    if i >= 3 - k:
                        down.append((j, k, off))

                def tile_up(j):
                    row = base + V_SLOTS[j][2] + i
                    return halves(jnp.where(px == 0, ra[row], rb[row]))

                def tile_down(j):
                    row = base + V_SLOTS[j][2] + i - (3 - V_SLOTS[j][1])
                    return halves(jnp.where(px == 0, rb[row], ra[row]))

                emit(d, CX + i, up, tile_up)
                emit(d, CX + 3 + i, down, tile_down)
            if with_image:
                own = refs[0]
                for i in range(4):
                    a, b = ra[FACE + i], rb[FACE + i]
                    other = own[12 + i] if d == 0 else jnp.where(px == d - 1, a, b)
                    pair = (halves(own[4 * d + i]), halves(other))
                    emit(d, VX + i, ((0, 4, 0), (1, 4, 4)), lambda key: pair[key])

    return pl.pallas_call(
        kernel,
        out_shape=[sds(3, rows, 8, NZ)] * 2,
        in_specs=[scalars()] + [whole()] * (4 if with_image else 3),
        out_specs=[whole()] * 2,
        compiler_params=params(),
    )(info, vt, ra, rb, *((tile,) if with_image else ()))


def forward_first(info, tile, vt, ra, rb, yc, yd):
    def kernel(info, tile, vt, ra, rb, yc, yd, pack, ea, eb, i4, vw, image, halos, hsem, sem, osem):
        px, py = info[2], info[3]
        pair = copies([(ra.at[FACE : FACE + DEPTH], halos.at[0]), (rb.at[FACE : FACE + DEPTH], halos.at[1])], hsem)
        started = fill_velocity(0, info, vt, ra, rb, yc, yd, vw, sem)
        image[0, 0:CX, 0:CY] = tile[...]
        wait_all(pair)
        image[0, pl.ds(jnp.where(px == 0, CX, WX - DEPTH), DEPTH), 0:CY] = halos[0]
        image[0, pl.ds(jnp.where(px == 0, WX - DEPTH, CX), DEPTH), 0:CY] = halos[1]
        sub = rows8()
        for j in range(12):
            c, e = yc[j // 4, VX + j % 4], yd[j // 4, VX + j % 4]
            above = jnp.where(py == 0, c, e)
            below = jnp.where(py == 0, e, c)
            image[0, j, CY:WY] = halo_block(above, below, 4, 0, sub)
            image[0, j + 12, CY:WY] = halo_block(above, below, 4, 4, sub)
        wait_all(started)
        out = []
        for j in range(4):
            advance(image.at[j], image.at[j + 1], vw, j, 3 - j)
            out.append(pltpu.make_async_copy(image.at[j, 0:CX, 0:CY], pack.at[j, 0:CX], osem.at[j]))
            out[-1].start()
        last = image.at[4]
        i4[...] = last[0:CX, 0:CY]
        ea[...] = last[pl.ds(jnp.where(px == 0, CX - DEPTH, 0), DEPTH), 0:CY]
        eb[...] = last[pl.ds(jnp.where(px == 0, 0, CX - DEPTH), DEPTH), 0:CY]
        wait_all(out)

    return pl.pallas_call(
        kernel,
        out_shape=[
            sds(NT, PBLOCKS, CY, NZ),
            sds(DEPTH, CY, NZ),
            sds(DEPTH, CY, NZ),
            sds(CX, CY, NZ),
            sds(4, 3, WX, WY, NZ),
        ],
        in_specs=[scalars()] + [whole()] * 6,
        out_specs=[hbm()] + [whole()] * 4,
        scratch_shapes=[
            VMEM((5, WX, WY, NZ), F32),
            VMEM((2, DEPTH, CY, NZ), F32),
            pltpu.SemaphoreType.DMA((2,)),
            pltpu.SemaphoreType.DMA((FILL_COPIES,)),
            pltpu.SemaphoreType.DMA((4,)),
        ],
        compiler_params=params(),
    )(info, tile, vt, ra, rb, yc, yd)


def window(info, vt, ra, rb, yc, yd, group):
    def kernel(info, vt, ra, rb, yc, yd, vw, sem):
        wait_all(fill_velocity(group, info, vt, ra, rb, yc, yd, vw, sem))

    return pl.pallas_call(
        kernel,
        out_shape=sds(4, 3, WX, WY, NZ),
        in_specs=[scalars()] + [whole()] * 5,
        out_specs=whole(),
        scratch_shapes=[pltpu.SemaphoreType.DMA((FILL_COPIES,))],
        compiler_params=params(),
    )(info, vt, ra, rb, yc, yd)


def send_rows(info, widths, source, ea, eb):
    px = info[2]
    off = 0
    for n, k in enumerate(widths):
        top = jnp.where(px == 0, CX, WX - k)
        bottom = jnp.where(px == 0, WX - k, CX)
        ea[off : off + k] = source(n)[pl.ds(top, k)]
        eb[off : off + k] = source(n)[pl.ds(bottom, k)]
        off += k


MID_WIDTHS = (4, 3, 2, 1)
MID_SLOTS = ((0, 4, 0), (1, 3, 4), (3, 1, 7))
END_WIDTHS = (3, 2, 1)
END_SLOTS = ((0, 3, 0), (1, 2, 3), (2, 1, 5), (3, 2, 6))


def forward_second(info, win, ic, idd, target, vw, pack, *before):
    def kernel(info, win, ic, idd, target, vw, pack_in, *refs):
        pack, lw, ea, eb, image, lam, osem = refs[len(before) :]
        fill_image(info, win, ic, idd, image.at[0])
        for n in range(4):
            clear_halo(lam.at[n])
        out = []
        for j in range(4):
            advance(image.at[j], image.at[j + 1], vw, j, 3 - j)
            out.append(pltpu.make_async_copy(image.at[j, 0:CX, 0:CY], pack.at[4 + j, 0:CX], osem.at[j]))
            out[-1].start()
        count = info[4]
        inside = lax.broadcasted_iota(jnp.int32, (CY, NZ), 0) * NZ + lax.broadcasted_iota(jnp.int32, (CY, NZ), 1)
        zero = jnp.zeros((8, NZ), F32)

        def one(x, carry):
            value = image[4, x, 0:CY] - target[x]
            lam[0, x, 0:CY] = jnp.where(inside + x * (CY * NZ) < count, value, 0.0)
            lam[0, x, CY:WY] = zero
            return carry

        lax.fori_loop(0, CX, one, 0)
        out.append(pltpu.make_async_copy(lam.at[0, 0:CX, 0:CY], pack.at[7, CX : 2 * CX], osem.at[4]))
        out[-1].start()
        for n in range(4):
            scatter(lam.at[n], lam.at[n + 1], vw, 3 - n, n + 1)
        for n in range(4):
            lw[n] = lam[4 - n, 0:CX]
        send_rows(info, MID_WIDTHS, lambda n: lam.at[4 - n], ea, eb)
        wait_all(out)

    return pl.pallas_call(
        kernel,
        out_shape=[sds(NT, PBLOCKS, CY, NZ), sds(4, CX, WY, NZ), sds(10, WY, NZ), sds(10, WY, NZ)],
        in_specs=[scalars()] + [whole()] * 5 + [hbm()] + [anywhere()] * len(before),
        out_specs=[hbm()] + [whole()] * 3,
        scratch_shapes=[
            VMEM((5, WX, WY, NZ), F32),
            VMEM((5, WX, WY, NZ), F32),
            pltpu.SemaphoreType.DMA((5,)),
        ],
        input_output_aliases={6: 0},
        compiler_params=params(),
    )(info, win, ic, idd, target, vw, pack, *before)


def costate_edges(info, lw, ra, rb, widths, slots, *before):
    def kernel(info, lw_in, ra, rb, *refs):
        lw, ec, ed = refs[len(before) :]
        px, py = info[2], info[3]
        off = 0
        for n, k in enumerate(widths):
            for i in range(k):
                to_a = jnp.where(px == 0, CX - k, 0) + i
                to_b = jnp.where(px == 0, 0, CX - k) + i
                lw[n, to_a] = lw[n, to_a] + ra[off + i]
                lw[n, to_b] = lw[n, to_b] + rb[off + i]
            off += k
        sub = rows8()

        def one(x, carry):
            top = jnp.zeros((8, NZ), F32)
            bottom = top
            for n, k, off in slots:
                block = lw[n, x, CY:WY]
                top = put(top, block, off, off, off + k, sub)
                bottom = put(bottom, block, off + k, off, off + k, sub)
            ec[x] = jnp.where(py == 0, top, bottom)
            ed[x] = jnp.where(py == 0, bottom, top)
            return carry

        lax.fori_loop(0, CX, one, 0)

    return pl.pallas_call(
        kernel,
        out_shape=[sds(4, CX, WY, NZ), sds(CX, 8, NZ), sds(CX, 8, NZ)],
        in_specs=[scalars()] + [whole()] * 3 + [anywhere()] * len(before),
        out_specs=[whole()] * 3,
        input_output_aliases={1: 0},
        compiler_params=params(),
    )(info, lw, ra, rb, *before)


def take(c, e, py, k, off, sub):
    below = jnp.where(py == 0, e, c)
    above = jnp.where(py == 0, c, e)
    zero = jnp.zeros((8, NZ), F32)
    return put(zero, below, -off, 0, k, sub), put(zero, above, 8 - k - off, 8 - k, 8, sub)


def backward_second(info, lw, lc, ld, vw, pack, *before):
    def kernel(info, lw, lc, ld, vw, pack_in, *refs):
        pack, lw2, ea, eb, lam, done, osem = refs[len(before) :]
        for n in range(3):
            clear_halo(lam.at[n])
        py = info[3]
        sub = rows8()
        zero = jnp.zeros((8, NZ), F32)

        def one(x, carry):
            c, e = lc[x], ld[x]
            for n, k, off in MID_SLOTS:
                low, high = take(c, e, py, k, off, sub)
                low, high = lw[n, x, 0:8] + low, lw[n, x, 8:16] + high
                if n == 0:
                    lam[0, x, 0:8] = low
                    lam[0, x, 8:16] = high
                    lam[0, x, CY:WY] = zero
                else:
                    done[(n - 1) // 2, x, 0:8] = low
                    done[(n - 1) // 2, x, 8:16] = high
            return carry

        lax.fori_loop(0, CX, one, 0)
        out = [
            pltpu.make_async_copy(lam.at[0, 0:CX, 0:CY], pack.at[3, CX : 2 * CX], osem.at[0]),
            pltpu.make_async_copy(done.at[0], pack.at[4, CX : 2 * CX], osem.at[1]),
            pltpu.make_async_copy(done.at[1], pack.at[6, CX : 2 * CX], osem.at[2]),
        ]
        for copy in out:
            copy.start()
        for n in range(3):
            scatter(lam.at[n], lam.at[n + 1], vw, 3 - n, n + 1)
        for n in range(3):
            lw2[n] = lam[3 - n, 0:CX]
        lw2[3] = lw[2]
        send_rows(info, END_WIDTHS, lambda n: lam.at[3 - n], ea, eb)
        wait_all(out)

    return pl.pallas_call(
        kernel,
        out_shape=[sds(NT, PBLOCKS, CY, NZ), sds(4, CX, WY, NZ), sds(6, WY, NZ), sds(6, WY, NZ)],
        in_specs=[scalars()] + [whole()] * 4 + [hbm()] + [anywhere()] * len(before),
        out_specs=[hbm()] + [whole()] * 3,
        scratch_shapes=[
            VMEM((4, WX, WY, NZ), F32),
            VMEM((2, CX, CY, NZ), F32),
            pltpu.SemaphoreType.DMA((3,)),
        ],
        input_output_aliases={5: 0},
        compiler_params=params(),
    )(info, lw, lc, ld, vw, pack, *before)


def costate_finish(info, lw, lc, ld, total, pack):
    def kernel(info, lw, lc, ld, total, pack_in, pack, done, note, sem):
        note[0] = jnp.broadcast_to(total[0:1], (CY, NZ))
        started = copies([(note, pack.at[t, 2 * CX : PBLOCKS]) for t in range(NT)], sem.at[pl.ds(4, NT)])
        py = info[3]
        sub = rows8()

        def one(x, carry):
            c, e = lc[x], ld[x]
            for n, k, off in END_SLOTS:
                low, high = take(c, e, py, k, off, sub)
                done[n, x, 0:8] = lw[n, x, 0:8] + low
                done[n, x, 8:16] = lw[n, x, 8:16] + high
            return carry

        lax.fori_loop(0, CX, one, 0)
        wait_all(copies([(done.at[n], pack.at[m, CX : 2 * CX]) for n, m in enumerate((0, 1, 2, 5))], sem))
        wait_all(started)

    return pl.pallas_call(
        kernel,
        out_shape=sds(NT, PBLOCKS, CY, NZ),
        in_specs=[scalars()] + [whole()] * 4 + [hbm()],
        out_specs=hbm(),
        scratch_shapes=[VMEM((4, CX, CY, NZ), F32), VMEM((1, CY, NZ), F32), pltpu.SemaphoreType.DMA((4 + NT,))],
        input_output_aliases={5: 0},
        compiler_params=params(58),
    )(info, lw, lc, ld, total, pack)


PAD = 8
PY = NY + 2 * PAD
CHUNK = 32


def clear_pads(ref, lead):
    zero = jnp.zeros((PAD, NZ), F32)
    for index in lead:
        ref[(*index, slice(0, PAD))] = zero
        ref[(*index, slice(PAD + NY, PY))] = zero


def part(ref, index, y, move=0):
    return ref[(*index, slice(PAD + y + move, PAD + y + move + CHUNK))]


def smooth(ref, before, at, after, y, m):
    first, last = m
    c = part(ref, at, y)
    near = part(ref, before, y) + part(ref, after, y)
    near += part(ref, at, y, -1) + part(ref, at, y, 1)
    near += jnp.where(first, 0.0, pltpu.roll(c, 1, 1)) + jnp.where(last, 0.0, pltpu.roll(c, NZ - 1, 1))
    return (1.0 - 6.0 * KAPPA) * c + KAPPA * near


def third_sum(c, beside):
    high = c.astype(jnp.bfloat16)
    low = (c - high.astype(F32)).astype(jnp.bfloat16)
    both = jnp.dot(jnp.concatenate([high, low], axis=0), beside, preferred_element_type=F32)
    return both[0 : c.shape[0]] + both[c.shape[0] :]


def smooth_rows(ref, x, rows, beside):
    inner = slice(PAD, PAD + NY)
    values = [ref[x + r, inner] for r in range(rows)]
    third = third_sum(jnp.concatenate(values, axis=0), beside)
    out = []
    for r, c in enumerate(values):
        near = third[r * NY : (r + 1) * NY] + ref[x + r - 1, inner] + ref[x + r + 1, inner]
        near += ref[x + r, PAD - 1 : PAD + NY - 1] + ref[x + r, PAD + 1 : PAD + NY + 1]
        out.append((1.0 - 6.0 * KAPPA) * c + KAPPA * near)
    return out


def slope(v, ref, before, at, after, direction, y, m):
    first, last = m
    c = part(ref, at, y)
    if direction == 0:
        behind, beyond = part(ref, before, y), part(ref, after, y)
    elif direction == 1:
        behind, beyond = part(ref, at, y, -1), part(ref, at, y, 1)
    else:
        behind = jnp.where(first, 0.0, pltpu.roll(c, 1, 1))
        beyond = jnp.where(last, 0.0, pltpu.roll(c, NZ - 1, 1))
    return jnp.where(v > 0.0, c - behind, beyond - c)


CHUNKS = tuple(range(0, NY, CHUNK))


def coefficient(notes, cells):
    total = notes[0, 0, 0:8]
    for c in range(1, NY // CY):
        total += notes[c, 0, 0:8]
    return ((-STEP * DATA_WEIGHT) * (cells / total))[0:1]


def finish_inside(velocity, pack, cells):
    def kernel(vel, pack, out, keep_c, keep_s, islab, lslab, grad, soft, notes, beside, sem):
        d = pl.program_id(0)

        @pl.when(d == 0)
        def _():
            pairs = []
            for c in range(NY // CY):
                y = slice(c * CY, (c + 1) * CY)
                padded = slice(PAD + c * CY, PAD + (c + 1) * CY)
                pairs += [
                    (pack.at[c, 0:CX], islab.at[:, padded]),
                    (pack.at[c, CX : 2 * CX], lslab.at[:, y]),
                    (pack.at[c, 2 * CX : PBLOCKS], notes.at[c]),
                ]
            started = copies(pairs, sem)
            apart = lax.broadcasted_iota(jnp.int32, (NZ, NZ), 0) - lax.broadcasted_iota(jnp.int32, (NZ, NZ), 1)
            beside[...] = jnp.where(jnp.abs(apart) == 1, 1.0, 0.0).astype(jnp.bfloat16)
            for ref in (islab, grad, soft):
                clear_pads(ref, [(x,) for x in range(CX)])
            wait_all(started)

        coef = coefficient(notes, cells)
        m = lane_masks((CHUNK, NZ))
        for direction in range(3):

            @pl.when(d == direction)
            def _(direction=direction):
                def one(x, carry):
                    for y in CHUNKS:
                        rows = slice(y, y + CHUNK)
                        g = slope(vel[0, 0, x, rows], islab, (x - 1,), (x,), (x + 1,), direction, y, m)
                        grad[x, PAD + y : PAD + y + CHUNK] = (coef * lslab[x, rows]) * g
                    return carry

                lax.fori_loop(1, CX - 1, one, 0)

        near = beside[...]

        def once(i, carry):
            x = 2 + 2 * i
            for r, value in enumerate(smooth_rows(grad, x, 2, near)):
                soft[x + r, PAD : PAD + NY] = value
            return carry

        lax.fori_loop(0, (CX - 4) // 2, once, 0)

        def twice(i, carry):
            x = 3 + 2 * i
            for r, value in enumerate(smooth_rows(soft, x, 2, near)):
                out[0, 0, x + r] = vel[0, 0, x + r] + value
            return carry

        lax.fori_loop(0, (CX - 6) // 2, twice, 0)
        for n, (x, y) in enumerate(((1, 2), (2, 3), (13, 12), (14, 13))):
            keep_c[0, n] = grad[x, PAD : PAD + NY]
            keep_s[0, n] = soft[y, PAD : PAD + NY]

    slab = pl.BlockSpec((1, 1, CX, NY, NZ), lambda d: (0, d, 0, 0, 0))
    kept = pl.BlockSpec((1, 4, NY, NZ), lambda d: (d, 0, 0, 0))
    return pl.pallas_call(
        kernel,
        grid=(3,),
        out_shape=[sds(1, 3, CX, NY, NZ), sds(3, 4, NY, NZ), sds(3, 4, NY, NZ)],
        in_specs=[slab, hbm()],
        out_specs=[slab, kept, kept],
        scratch_shapes=[VMEM((CX, PY, NZ), F32), VMEM((CX, NY, NZ), F32), VMEM((CX, PY, NZ), F32), VMEM((CX, PY, NZ), F32)]
        + [VMEM((8, 1, CY, NZ), F32), VMEM((NZ, NZ), jnp.bfloat16), pltpu.SemaphoreType.DMA((24,))],
        compiler_params=params(60),
    )(velocity, pack)


def finish_edges(info, velocity, va, vb, pack, fa, fb, keep_c, keep_s, partial, cells):
    def kernel(info, vel, va, vb, pack, fa, fb, keep_c, keep_s, partial, out, slabs, all_rows, grad, soft, all_results, notes, sem, osem):
        d = pl.program_id(0)
        px = info[2]

        @pl.when(d == 0)
        def _():
            pairs = []
            above, below = jnp.where(px == 0, 1, 0), jnp.where(px == 0, 0, 1)
            hi, hl = jnp.where(px == 0, 2, 0), jnp.where(px == 0, 6, 5)
            bi, bl = jnp.where(px == 0, 0, 2), jnp.where(px == 0, 5, 6)
            for c in range(NY // CY):
                y = slice(PAD + c * CY, PAD + (c + 1) * CY)
                pairs += [
                    (pack.at[c, 0:2], slabs.at[0, 3:5, y]),
                    (pack.at[c, CX : CX + 1], slabs.at[0, 7:8, y]),
                    (pack.at[c, CX - 2 : CX], slabs.at[1, 0:2, y]),
                    (pack.at[c, 2 * CX - 1 : 2 * CX], slabs.at[1, 5:6, y]),
                    (pack.at[c, 2 * CX : PBLOCKS], notes.at[c]),
                    (fa.at[c, 0:3], slabs.at[above, pl.ds(hi, 3), y]),
                    (fa.at[c, 3:5], slabs.at[above, pl.ds(hl, 2), y]),
                    (fb.at[c, 0:3], slabs.at[below, pl.ds(bi, 3), y]),
                    (fb.at[c, 3:5], slabs.at[below, pl.ds(bl, 2), y]),
                ]
            for n in range(3):
                pairs += [(vel.at[0, n, 0:3], all_rows.at[n, 0]), (vel.at[0, n, CX - 3 : CX], all_rows.at[n, 1])]
            started = copies(pairs, sem)
            clear_pads(slabs, [(side, n) for side in range(2) for n in range(5)])
            for ref in (grad, soft):
                clear_pads(ref, [(side, n) for side in range(2) for n in range(5)])
            wait_all(started)

        vrows, result = all_rows.at[d], all_results.at[d]

        coef = coefficient(notes, cells)
        m = lane_masks((CHUNK, NZ))
        for direction in range(3):

            @pl.when(d == direction)
            def _(direction=direction):
                for side in range(2):
                    for n in range(3):
                        own = n == 2 if side == 0 else n == 0
                        for y in CHUNKS:
                            rows = slice(y, y + CHUNK)
                            if own:
                                v = vrows[0, 0, rows] if side == 0 else vrows[1, 2, rows]
                            else:
                                k = n if side == 0 else n - 1
                                v = jnp.where((px == 0) == (side == 1), va[0, k, rows], vb[0, k, rows])
                            g = slope(v, slabs, (side, n), (side, n + 1), (side, n + 2), direction, y, m)
                            grad[side, n, PAD + y : PAD + y + CHUNK] = (coef * part(slabs, (side, 5 + n), y)) * g

        inner = slice(PAD, PAD + NY)
        for n in range(2):
            grad[0, 3 + n, inner] = keep_c[0, n]
            grad[1, 3 + n, inner] = keep_c[0, 2 + n]
            soft[0, 3 + n, inner] = keep_s[0, n]
            soft[1, n, inner] = keep_s[0, 2 + n]
        zero = jnp.zeros((NY, NZ), F32)
        for side in range(2):
            order = [0, 1, 2, 3, 4] if side == 0 else [3, 4, 0, 1, 2]
            for n in range(3):
                at = [(side, order[n + k]) for k in range(3)]
                for y in CHUNKS:
                    soft[side, n + 2 * side, PAD + y : PAD + y + CHUNK] = smooth(grad, *at, y, m)

        @pl.when(info[0] == 0)
        def _():
            soft[0, 0, inner] = zero

        @pl.when(info[0] == info[5] - 1)
        def _():
            soft[1, 4, inner] = zero

        for side in range(2):
            for n in range(3):
                for y in CHUNKS:
                    rows = slice(y, y + CHUNK)
                    value = smooth(soft, (side, n), (side, n + 1), (side, n + 2), y, m)
                    result[side, n, rows] = vrows[side, n, rows] + value

        def leave(n):
            low, high = all_results.at[n, 0], all_results.at[n, 1]
            return [
                pltpu.make_async_copy(low, out.at[0, n, 0:3], osem.at[n, 0]),
                pltpu.make_async_copy(high, out.at[0, n, CX - 3 : CX], osem.at[n, 1]),
            ]

        for n in range(3):

            @pl.when(d == n)
            def _(n=n):
                for copy in leave(n):
                    copy.start()

        @pl.when(d == 2)
        def _():
            for n in range(3):
                wait_all(leave(n))

    face = pl.BlockSpec((1, 2, NY, NZ), lambda d: (d, 0, 0, 0))
    kept = pl.BlockSpec((1, 4, NY, NZ), lambda d: (d, 0, 0, 0))
    return pl.pallas_call(
        kernel,
        grid=(3,),
        out_shape=sds(1, 3, CX, NY, NZ),
        in_specs=[scalars(), hbm(), face, face] + [hbm()] + [anywhere()] * 2 + [kept, kept, hbm()],
        out_specs=hbm(),
        scratch_shapes=[
            VMEM((2, 8, PY, NZ), F32),
            VMEM((3, 2, 3, NY, NZ), F32),
            VMEM((2, 5, PY, NZ), F32),
            VMEM((2, 5, PY, NZ), F32),
            VMEM((3, 2, 3, NY, NZ), F32),
            VMEM((8, 1, CY, NZ), F32),
            pltpu.SemaphoreType.DMA((78,)),
            pltpu.SemaphoreType.DMA((3, 2)),
        ],
        input_output_aliases={9: 0},
        compiler_params=params(60),
    )(info, velocity, va, vb, pack, fa, fb, keep_c, keep_s, partial)


def edge_rows(value, dim, k, px):
    length = value.shape[dim]
    high = lax.slice_in_dim(value, length - k, length, axis=dim)
    low = lax.slice_in_dim(value, 0, k, axis=dim)
    return jnp.where(px == 0, high, low), jnp.where(px == 0, low, high)


def shards(velocity, atlas_image, target, labels, label_table, counts):
    s, c = lax.axis_index("space"), lax.axis_index("cuts")
    px, py = s % 2, c % 2
    info = jnp.stack([s, c, px, py, counts[0], jnp.int32(lax.axis_size("space")), s, s]).astype(jnp.int32)
    far_a, far_b, *direct = repack(info, velocity)
    got, far = spread(far_a, far_b, direct[:5])

    tile, ova, ovb = template(info, label_table, atlas_image, labels, velocity, far)
    ova, ovb = swap(ova, ovb, "space")

    vt, fa, fb, ga, gb, total = faces(info, direct[5], got, tile, ova, ovb)
    fa, fb = swap(fa, fb, "space")
    ga, gb = swap(ga, gb, "space")
    y0 = swap(*velocity_edges(info, vt, fa, fb, 0, tile), "cuts")
    total = xor_swap(total, 1)
    y1 = swap(*velocity_edges(info, vt, ga, gb, 1), "cuts")
    pack, ea, eb, i4, vw0 = forward_first(info, tile, vt, fa, fb, *y0)
    win, ec, ed = image_edges(info, i4, *swap(ea, eb, "space"))
    vw1 = window(info, vt, ga, gb, *y1, 1)
    ic, idd = swap(ec, ed, "cuts")
    pack, lw, ea, eb = forward_second(info, win, ic, idd, target, vw1, pack, total)
    total = xor_swap(total, 2)
    lw, ec, ed = costate_edges(info, lw, *swap(ea, eb, "space"), MID_WIDTHS, MID_SLOTS, total)
    total = xor_swap(total, 4)
    ec, ed = swap(ec, ed, "cuts")
    pack, lw, ea, eb = backward_second(info, lw, ec, ed, vw0, pack, total)
    total = xor_swap(total, 8)
    lw, ec, ed = costate_edges(info, lw, *swap(ea, eb, "space"), END_WIDTHS, END_SLOTS)
    ec, ed = swap(ec, ed, "cuts")
    pack = costate_finish(info, lw, ec, ed, total, pack)
    pack = lax.all_to_all(pack, "cuts", split_axis=0, concat_axis=0, tiled=True)

    cells = float(CX * CY * NZ * lax.axis_size("space") * lax.axis_size("cuts"))
    rows = [jnp.concatenate([pack[:, a : a + 3], pack[:, b : b + 2]], axis=1) for a, b in ((CX - 3, 2 * CX - 2), (0, CX))]
    ea, eb = jnp.where(px == 0, rows[0], rows[1]), jnp.where(px == 0, rows[1], rows[0])
    fa, fb = swap(ea, eb, "space")
    partial, keep_c, keep_s = finish_inside(velocity, pack, cells)
    return finish_edges(info, velocity, ova, ovb, pack, fa, fb, keep_c, keep_s, partial, cells)


def solution(mesh):
    in_specs = (
        P("cuts", None, "space", None, None),
        P("space", "cuts", None),
        P("space", "cuts", None),
        P("space", "cuts", None),
        P(),
        P(("space", "cuts")),
    )
    out_specs = P("cuts", None, "space", None, None)
    return jax.shard_map(shards, mesh=mesh, in_specs=in_specs, out_specs=out_specs, check_vma=False)
```
